256 devices in a mesh: dp: 8 (over z), phase: 4 (over y), dom: 8 (over x, core).
Axes of the slice: x: 4, y: 4, z: 8, core: 2. Of those that a mesh axis runs over, the one named last changes fastest.
Arguments:
- initial: bfloat16 [32, 2048, 256], P('dp', 'dom'), may hold values from -6 to 6
- block_cols: int32 [32, 16, 5], P('dp', 'dom'), may hold values from 0 to 15, as said below
- block_tiles: bfloat16 [32, 16, 5, 128, 128], P('dp', 'dom')
- layer_weights: bfloat16 [4, 256, 256], P('phase'), may hold values from -0.375 to 0.375
- cotangent: bfloat16 [32, 2048, 256], P('dp', 'dom'), may hold values from -6 to 6
Outputs:
- grad_initial: float32 [32, 2048, 256], P(('dp', 'phase'), 'dom')
- grad_weights: float32 [4, 256, 256], P('phase')
The draws below stay inside these ranges and needn't reach their ends.
Inputs may be any that keep to these rules, and one draw needn't show every extreme that they name: `block_cols`: in every span the matrix P_c is symmetric, and slot 0 of each block row names that block row itself.
All inputs are finite; a program needn't handle non-finite values.
Results may differ from the reference program's by a relative error of at most 0.008.
Values may be sent and summed in bfloat16 or wider, within the bound.
No kernel may reach another device: no remote copies, remote signals or barrier semaphores. Data moves between devices by JAX's collectives and lax.ppermute only.
A program may use at most 64 MiB of HBM per device.

```python
import math
import jax
import jax.numpy as jnp
from jax import lax

WIDTH = 256
BLK = 128
NZB = 5
NB = 16
NODES = 2048
SPANS = 32
LAYERS = 4


def block_pattern(key):
    span_keys = jax.random.split(key, SPANS)

    def per_span(span_key):
        key_shift, key_order = jax.random.split(span_key)
        offsets_half = jax.random.randint(key_shift, (NZB // 2,), 1, NB)
        ordering = jax.random.permutation(key_order, NB)
        return (ordering.astype(jnp.int32), offsets_half.astype(jnp.int32))
    return jax.vmap(per_span)(span_keys)


def draw_block_cols(key, part):
    orderings, offsets_all = block_pattern(key)

    def per_span(ordering, offsets_half):
        signed = jnp.stack([offsets_half, -offsets_half], axis=1).reshape(-1)
        offsets = jnp.concatenate([jnp.zeros((1,), jnp.int32), signed])
        position = jnp.arange(NB, dtype=jnp.int32)
        targets = ordering[(position[:, None] + offsets[None, :]) % NB]
        return targets[jnp.argsort(ordering)]
    return jax.vmap(per_span)(orderings, offsets_all).astype(jnp.int32)


def draw_block_tiles(key, part):
    orderings, offsets_all = block_pattern(key)
    key = jax.random.fold_in(key, 5)
    spread = 0.6 / math.sqrt(NZB * BLK)
    tile_shape = (SPANS, NB, NZB // 2 + 1, BLK, BLK)
    source_all = jax.random.normal(key, tile_shape, jnp.float32) * spread

    def per_span(ordering, offsets_half, source):
        diagonal = (source[:, 0] + jnp.swapaxes(source[:, 0], -1, -2)) * 0.70710678
        position = jnp.arange(NB, dtype=jnp.int32)
        members = [diagonal]
        for pair_idx in range(NZB // 2):
            ahead = source[:, pair_idx + 1]
            behind = jnp.swapaxes(ahead[(position - offsets_half[pair_idx]) % NB], -1, -2)
            members.append(ahead)
            members.append(behind)
        stacked = jnp.stack(members, axis=1)
        return stacked[jnp.argsort(ordering)]
    return jax.vmap(per_span)(orderings, offsets_all, source_all).astype(jnp.bfloat16)


def level_of(own_key, extent, cuts, low, top_value):
    def one(dim, blocks):
        heights = jax.random.uniform(jax.random.fold_in(jax.random.fold_in(own_key, 6), dim), (blocks,), jnp.float32, low / len(cuts), top_value / len(cuts))
        return jnp.repeat(jnp.exp(heights), extent[dim] // blocks).reshape((-1,) + (1,) * (len(extent) - dim - 1))

    level = one(*cuts[0])
    for cut in cuts[1:]:
        level = level * one(*cut)
    return level


def noise(own_key, extent, width, most, cuts=(), kind=jnp.bfloat16):
    values = width * jax.random.normal(own_key, extent, jnp.float32)
    if cuts:
        values = values * level_of(own_key, extent, cuts, -0.22, 0.18)
    return jnp.clip(values, -most, most).astype(kind)


def setup_inputs(seed: int = 0) -> dict:
    keys = jax.random.split(jax.random.key(seed), 6)
    return {
        "initial": noise(keys[0], (SPANS, NODES, WIDTH), 1.0, 6.0, ((0, 8), (1, 8))),
        "block_cols": draw_block_cols(jax.random.fold_in(keys[5], 71), 0),
        "block_tiles": draw_block_tiles(jax.random.fold_in(keys[5], 71), 0),
        "layer_weights": noise(keys[3], (LAYERS, WIDTH, WIDTH), WIDTH ** -0.5, 0.375, ((0, 4),)),
        "cotangent": noise(keys[4], (SPANS, NODES, WIDTH), 1.0, 6.0, ((0, 8), (1, 8))),
    }


alpha_mix = 0.1
theta_coef = 0.5

def gelu_tanh(inputs):
    return jax.nn.gelu(inputs, approximate=True)

def reference(initial, block_cols, block_tiles, layer_weights, cotangent):
    span_total, node_total, feat_width = initial.shape
    block_rows = block_tiles.shape[-1]
    layer_total = layer_weights.shape[0]
    grad_scale = 1.0 / math.sqrt(span_total * node_total)
    beta_table = jnp.log(theta_coef / (jnp.arange(layer_total).astype(jnp.float32) + 1.0) + 1.0)

    def aggregate(tiles_c, cols_c, rows_in):
        blocks = rows_in.reshape(-1, block_rows, feat_width).astype(jnp.float32)[cols_c]
        result = jnp.einsum('ikrc,ikch->irh', tiles_c.astype(jnp.float32), blocks)
        return result.reshape(-1, feat_width)

    def transpose_aggregate(tiles_c, cols_c, rows_in):
        pieces = rows_in.reshape(-1, block_rows, feat_width).astype(jnp.float32)
        contrib = jnp.einsum('ikrc,irh->ikch', tiles_c.astype(jnp.float32), pieces)
        full_rows = jnp.zeros(pieces.shape, jnp.float32).at[cols_c].add(contrib)
        return full_rows.reshape(-1, feat_width)

    def one_span(grad_acc, inputs):
        start_c, cols_c, tiles_c, cot_c = inputs
        hidden_state = start_c
        mixes = []
        pres = []
        for layer_idx in range(layer_total):
            beta_now = beta_table[layer_idx]
            aggregated = aggregate(tiles_c, cols_c, hidden_state)
            mix_rows = ((1.0 - alpha_mix) * aggregated + alpha_mix * start_c.astype(jnp.float32)).astype(jnp.bfloat16)
            pre_act = (1.0 - beta_now) * mix_rows.astype(jnp.float32) + beta_now * jnp.dot(mix_rows, layer_weights[layer_idx], preferred_element_type=jnp.float32)
            hidden_state = gelu_tanh(pre_act).astype(jnp.bfloat16)
            mixes.append(mix_rows)
            pres.append(pre_act)
        hidden_grad = cot_c
        grad_start = jnp.zeros(start_c.shape, jnp.float32)
        terms = [None] * layer_total
        for layer_idx in reversed(range(layer_total)):
            beta_now = beta_table[layer_idx]
            _, pullback = jax.vjp(gelu_tanh, pres[layer_idx])
            grad_pre = pullback(hidden_grad.astype(jnp.float32))[0].astype(jnp.bfloat16)
            terms[layer_idx] = beta_now * grad_scale * jnp.dot(mixes[layer_idx].T, grad_pre, preferred_element_type=jnp.float32)
            grad_mix = ((1.0 - beta_now) * grad_pre.astype(jnp.float32) + beta_now * jnp.dot(grad_pre, layer_weights[layer_idx].T, preferred_element_type=jnp.float32)).astype(jnp.bfloat16)
            grad_start = grad_start + alpha_mix * grad_mix.astype(jnp.float32)
            hidden_grad = ((1.0 - alpha_mix) * transpose_aggregate(tiles_c, cols_c, grad_mix)).astype(jnp.bfloat16)
        grad_start = grad_start + hidden_grad.astype(jnp.float32)
        return (grad_acc + jnp.stack(terms), grad_start)
    zeros_w = jnp.zeros((layer_total, feat_width, feat_width), jnp.float32)
    grad_weights, grad_initial = lax.scan(one_span, zeros_w, (initial, block_cols, block_tiles, cotangent))
    return (grad_initial, grad_weights)
```

```python
import functools
import math

import jax
import jax.numpy as jnp
from jax import lax
from jax.experimental import pallas as pl
from jax.experimental.pallas import tpu as pltpu
from jax.sharding import PartitionSpec as P

ALPHA = 0.1
THETA = 0.5
BLK = 128
NZB = 5
GELU_C = math.sqrt(2.0 / math.pi)
GELU_B = 0.044715
HEAD_TILES = 7
BF16 = jnp.bfloat16
F32 = jnp.float32


def pack_kernel(tiles, initial, cotangent, cols, head, tail, cot, cols_vec, sems):
    span = lax.axis_index("phase")
    lane = lax.broadcasted_iota(jnp.int32, cols_vec.shape, 1)
    vec = jnp.zeros(cols_vec.shape, F32)
    for b in range(2):
        for k in range(NZB):
            vec = jnp.where(lane == b * NZB + k, cols[span, b, k].astype(F32), vec)
    cols_vec[...] = vec.astype(BF16)
    rest = 2 * NZB - HEAD_TILES
    base = rest * BLK
    copies = [
        (tiles.at[span, pl.ds(0, HEAD_TILES)], head),
        (initial.at[span, :, pl.ds(0, BLK)], tail.at[pl.ds(base, 256)]),
        (initial.at[span, :, pl.ds(BLK, BLK)], tail.at[pl.ds(base + 256, 256)]),
        (cols_vec, tail.at[pl.ds(base + 512, 16)]),
        (cotangent.at[span], cot),
    ]
    for t in range(rest):
        copies.append((tiles.at[span, HEAD_TILES + t], tail.at[pl.ds(t * BLK, BLK)]))
    started = [pltpu.make_async_copy(a, b, sems.at[n]) for n, (a, b) in enumerate(copies)]
    for c in started:
        c.start()
    for c in started:
        c.wait()


def pack(tiles, initial, cotangent, cols):
    rest = 2 * NZB - HEAD_TILES
    any_spec = pl.BlockSpec(memory_space=pl.ANY)
    return pl.pallas_call(
        pack_kernel,
        in_specs=[any_spec, any_spec, any_spec, pl.BlockSpec(memory_space=pltpu.SMEM)],
        out_specs=[any_spec] * 3,
        out_shape=[
            jax.ShapeDtypeStruct((HEAD_TILES, BLK, BLK), BF16),
            jax.ShapeDtypeStruct((rest * BLK + 512 + 16, BLK), BF16),
            jax.ShapeDtypeStruct((256, 256), BF16),
        ],
        scratch_shapes=[pltpu.VMEM((16, BLK), BF16), pltpu.SemaphoreType.DMA((5 + rest,))],
        name="pack",
    )(tiles, initial, cotangent, cols)


def dot(a, b, dims):
    return lax.dot_general(a, b, (dims, ((), ())), preferred_element_type=F32)


def layers_kernel(scale, betas, *refs):
    heads, tails, cots, weights = refs[0:8], refs[8:16], refs[16:24], refs[24:28]
    grad_initial, grad_weights = refs[28:30]
    tiles, start, cot, weight, cols_bf, cols_int, cols, h_a, h_b, mixes, slopes, dpre, dw, sems = refs[30:]
    dom = lax.axis_index("dom")
    phase = lax.axis_index("phase")
    x, core = dom // 2, dom % 2
    rest = 2 * NZB - HEAD_TILES
    base = rest * BLK
    layers = weights_n = 4
    slots = [((x - n // 2 + 4) % 4) * 2 + (core if n % 2 == 0 else 1 - core) for n in range(8)]
    copies = []
    for n in range(8):
        s = slots[n]
        copies.append((tails[n].at[pl.ds(base + 512, 16)], cols_bf.at[pl.ds(s * 16, 16)]))
    for n in range(8):
        s = slots[n]
        copies.append((heads[n], tiles.at[pl.ds(s * 10, HEAD_TILES)]))
        for t in range(rest):
            copies.append((tails[n].at[pl.ds(t * BLK, BLK)], tiles.at[s * 10 + HEAD_TILES + t]))
        rows = pl.ds(pl.multiple_of(s * 256, 256), 256)
        copies.append((tails[n].at[pl.ds(base, 256)], start.at[rows, pl.ds(0, BLK)]))
        copies.append((tails[n].at[pl.ds(base + 256, 256)], start.at[rows, pl.ds(BLK, BLK)]))
        copies.append((cots[n], cot.at[rows]))
    for n in range(weights_n):
        copies.append((weights[n].at[0], weight.at[(phase - n + 4) % 4]))
    started = [pltpu.make_async_copy(a, b, sems.at[n]) for n, (a, b) in enumerate(copies)]
    for c in started:
        c.start()
    for c in started[:8]:
        c.wait()
    cols_int[...] = cols_bf[...].astype(F32).astype(jnp.int32)
    last = pltpu.make_async_copy(cols_int, cols, sems.at[len(copies)])
    last.start()
    last.wait()
    for c in started[8:]:
        c.wait()

    def aggregate(source, i):
        part, b = i // 2, i % 2
        blocks = []
        for k in range(NZB):
            j = cols[part * 16, b * NZB + k]
            blocks.append(source[pl.ds(pl.multiple_of(j * BLK, BLK), BLK), :])
        t = [tiles[i * NZB + k] for k in range(NZB)]
        return dot(jnp.concatenate(t, axis=1), jnp.concatenate(blocks, axis=0), ((1,), (0,)))

    nodes = start.shape[0]
    buffers = (h_a, h_b)
    source = start
    for l in range(layers):
        target = buffers[l % 2]
        beta = betas[l]

        def forward(i, _, source=source, target=target, beta=beta, l=l):
            rows = pl.ds(pl.multiple_of(i * BLK, BLK), BLK)
            agg = aggregate(source, i)
            mix = ((1.0 - ALPHA) * agg + ALPHA * start[rows, :].astype(F32)).astype(BF16)
            mixes[l, rows, :] = mix
            pre = (1.0 - beta) * mix.astype(F32) + beta * dot(mix, weight[l], ((1,), (0,)))
            square = pre * pre
            t = jnp.tanh(pre * (GELU_C + (GELU_C * GELU_B) * square))
            half = 0.5 + 0.5 * t
            hidden = pre * half
            if l < layers - 1:
                target[rows, :] = hidden.astype(BF16)
            slopes[l, rows, :] = half + hidden * (1.0 - half) * (
                2.0 * GELU_C + (6.0 * GELU_C * GELU_B) * square
            )
            return 0

        lax.fori_loop(0, nodes // BLK, forward, 0)
        source = target

    own = pl.ds(pl.multiple_of(dom * 256, 256), 256)
    source = None
    for l in reversed(range(layers)):
        target = buffers[l % 2]
        beta = betas[l]

        def backward(i, _, source=source, target=target, beta=beta, l=l):
            rows = pl.ds(pl.multiple_of(i * BLK, BLK), BLK)
            if source is None:
                back = cot[rows, :]
            else:
                back = ((1.0 - ALPHA) * aggregate(source, i)).astype(BF16)
            grad = (slopes[l, rows, :] * back.astype(F32)).astype(BF16)
            dpre[rows, :] = grad
            dmix = (1.0 - beta) * grad.astype(F32) + beta * dot(grad, weight[l], ((1,), (1,)))
            target[rows, :] = dmix.astype(BF16)
            return 0

        lax.fori_loop(0, nodes // BLK, backward, 0)
        term = ALPHA * target[own, :].astype(F32)
        grad_initial[0] = term if l == layers - 1 else grad_initial[0] + term
        dw[...] = (beta * scale) * dot(mixes[l], dpre[...], ((0,), (0,)))
        grad_weights[l] = dw[pl.ds(pl.multiple_of(dom * 32, 32), 32), :]
        source = target
    for b in range(2):
        last_back = ((1.0 - ALPHA) * aggregate(source, dom * 2 + b)).astype(BF16)
        rows = pl.ds(b * BLK, BLK)
        grad_initial[0, rows, :] = grad_initial[0, rows, :] + last_back.astype(F32)


def run_layers(scale, betas, heads, tails, cots, weights):
    any_spec = pl.BlockSpec(memory_space=pl.ANY)
    vmem = pl.BlockSpec(memory_space=pltpu.VMEM)
    nodes, width = 2048, 256
    return pl.pallas_call(
        functools.partial(layers_kernel, scale, betas),
        in_specs=[any_spec] * 28,
        out_specs=[vmem, vmem],
        out_shape=[
            jax.ShapeDtypeStruct((1, 256, width), F32),
            jax.ShapeDtypeStruct((4, 32, width), F32),
        ],
        scratch_shapes=[
            pltpu.VMEM((80, BLK, BLK), BF16),
            pltpu.VMEM((nodes, width), BF16),
            pltpu.VMEM((nodes, width), BF16),
            pltpu.VMEM((4, width, width), BF16),
            pltpu.VMEM((8 * 16, BLK), BF16),
            pltpu.VMEM((8 * 16, BLK), jnp.int32),
            pltpu.SMEM((8 * 16, BLK), jnp.int32),
            pltpu.VMEM((nodes, width), BF16),
            pltpu.VMEM((nodes, width), BF16),
            pltpu.VMEM((4, nodes, width), BF16),
            pltpu.VMEM((4, nodes, width), F32),
            pltpu.VMEM((nodes, width), BF16),
            pltpu.VMEM((width, width), F32),
            pltpu.SemaphoreType.DMA((8 * 8 + 8,)),
        ],
        compiler_params=pltpu.CompilerParams(vmem_limit_bytes=48 * 1024 * 1024),
        cost_estimate=pl.CostEstimate(flops=9_000_000_000, bytes_accessed=6_000_000, transcendentals=0),
        name="layers",
    )(*heads, *tails, *cots, *weights)


def ring(v, step):
    return lax.ppermute(v, "dom", [(i, (i + 2 * step) % 8) for i in range(8)])


def other_core(v):
    return lax.ppermute(v, "dom", [(i, i ^ 1) for i in range(8)])


def gather(v, way):
    from_left, from_right = ring(v, 1), ring(v, -1)
    far = ring(from_left, 1) if way > 0 else ring(from_right, -1)
    pieces = []
    for piece in (v, from_left, far, from_right):
        pieces += [piece, other_core(piece)]
    return pieces


def local(initial, block_cols, block_tiles, layer_weights, cotangent):
    layers = lax.axis_size("phase")
    nodes_all = 4 * 2048 * lax.axis_size("dp")
    scale = 1.0 / math.sqrt(nodes_all)
    betas = [math.log(THETA / (l + 1) + 1.0) for l in range(layers)]
    spans, rows = block_tiles.shape[:2]
    tiles = block_tiles.reshape(spans, rows * NZB, BLK, BLK)
    head, tail, cot = pack(tiles, initial, cotangent, block_cols)
    heads = gather(head, 1)
    tails = gather(tail, -1)
    weights = [layer_weights] + [
        lax.ppermute(layer_weights, "phase", [(i, (i + n) % 4) for i in range(4)]) for n in (1, 2, 3)
    ]
    cots = gather(cot, 1)
    grad_initial, parts = run_layers(scale, betas, heads, tails, cots, weights)
    parts = lax.all_to_all(parts, "phase", 0, 0, tiled=True)
    mine = jnp.sum(parts, axis=0)
    mine = jnp.broadcast_to(mine[None], (8,) + mine.shape)
    mine = jnp.sum(lax.all_to_all(mine, "dp", 0, 0, tiled=True), axis=0)
    mine = jnp.broadcast_to(mine[None], (8,) + mine.shape)
    mine = lax.all_to_all(mine, "dom", 0, 0, tiled=True)
    return grad_initial, mine.reshape(1, 256, 256)


def solution(mesh):
    placed = (
        P("dp", "dom", None),
        P("dp", "dom", None),
        P("dp", "dom", None, None, None),
        P("phase", None, None),
        P("dp", "dom", None),
    )
    return jax.shard_map(
        local,
        mesh=mesh,
        in_specs=placed,
        out_specs=(P(("dp", "phase"), "dom", None), P("phase", None, None)),
        check_vma=False,
    )
```

```python
import functools
import math

import jax
import jax.numpy as jnp
from jax import lax
from jax.experimental import pallas as pl
from jax.experimental.pallas import tpu as pltpu
from jax.sharding import PartitionSpec as P

ALPHA = 0.1
THETA = 0.5
BLK = 128
NZB = 5
GELU_C = math.sqrt(2.0 / math.pi)
GELU_B = 0.044715
HEAD_TILES = 7
TAIL_START = (2 * NZB - HEAD_TILES) * BLK
TAIL_COLS = TAIL_START + 512
CHUNK = 4
BF16 = jnp.bfloat16
F32 = jnp.float32


def pack_kernel(tiles, initial, cotangent, cols, head, tail, cot, start, sems):
    span = lax.axis_index("phase")
    rest = 2 * NZB - HEAD_TILES
    copies = [
        (tiles.at[span, pl.ds(0, HEAD_TILES)], head),
        (initial.at[span], start),
        (cotangent.at[span], cot),
    ]
    for t in range(rest):
        copies.append((tiles.at[span, HEAD_TILES + t], tail.at[pl.ds(t * BLK, BLK)]))
    started = [pltpu.make_async_copy(a, b, sems.at[n]) for n, (a, b) in enumerate(copies)]
    for c in started:
        c.start()
    lane = lax.broadcasted_iota(jnp.int32, (16, BLK), 1)
    vec = jnp.zeros((16, BLK), F32)
    for b in range(2):
        for k in range(NZB):
            vec = jnp.where(lane == b * NZB + k, cols[span, b, k].astype(F32), vec)
    tail[TAIL_COLS : TAIL_COLS + 16, :] = vec.astype(BF16)
    for c in started:
        c.wait()
    tail[TAIL_START : TAIL_START + 256, :] = start[:, :BLK]
    tail[TAIL_START + 256 : TAIL_START + 512, :] = start[:, BLK:]


def pack(tiles, initial, cotangent, cols):
    rest = 2 * NZB - HEAD_TILES
    any_spec = pl.BlockSpec(memory_space=pl.ANY)
    vmem = pl.BlockSpec(memory_space=pltpu.VMEM)
    return pl.pallas_call(
        pack_kernel,
        in_specs=[any_spec, any_spec, any_spec, pl.BlockSpec(memory_space=pltpu.SMEM)],
        out_specs=[vmem] * 3,
        out_shape=[
            jax.ShapeDtypeStruct((HEAD_TILES, BLK, BLK), BF16),
            jax.ShapeDtypeStruct((TAIL_COLS + 16, BLK), BF16),
            jax.ShapeDtypeStruct((256, 256), BF16),
        ],
        scratch_shapes=[pltpu.VMEM((256, 256), BF16), pltpu.SemaphoreType.DMA((3 + rest,))],
        name="pack",
    )(tiles, initial, cotangent, cols)


def dot(a, b, dims):
    return lax.dot_general(a, b, (dims, ((), ())), preferred_element_type=F32)


def layers_kernel(scale, betas, *refs):
    heads, tails, cots, weights = refs[0:8], refs[8:16], refs[16:24], refs[24:28]
    grad_initial, grad_weights = refs[28:30]
    start, weight, cols_int, cols, hidden, mixes, slopes, dpre, dw, sem = refs[30:]
    dom = lax.axis_index("dom")
    phase = lax.axis_index("phase")
    x, core = dom // 2, dom % 2
    layers = len(weights)
    for n in range(8):
        j = tails[n][TAIL_COLS : TAIL_COLS + 16, :].astype(F32).astype(jnp.int32)
        chip = lax.bitwise_and(x - lax.shift_right_logical(j, 2) + 4, 3)
        side = lax.bitwise_xor(lax.bitwise_and(lax.shift_right_logical(j, 1), 1), core)
        place = chip * 4 + side * 2 + lax.bitwise_and(j, 1)
        cols_int[n : n + 1, :] = (place * BLK)[:1]
    to_scalars = pltpu.make_async_copy(cols_int, cols, sem)
    to_scalars.start()
    for n in range(8):
        for half in range(2):
            part = tails[n][TAIL_START + 256 * half : TAIL_START + 256 * (half + 1), :]
            lanes = slice(BLK * half, BLK * (half + 1))
            hidden[0, 256 * n : 256 * (n + 1), lanes] = part
            start[256 * n : 256 * (n + 1), lanes] = ALPHA * part.astype(F32)
    for n in range(layers):
        weight[(phase - n + layers) % layers] = weights[n][0]
    to_scalars.wait()

    def tile(i, k):
        n, t = i // 2, (i % 2) * NZB + k
        if t < HEAD_TILES:
            return heads[n][t]
        return tails[n][(t - HEAD_TILES) * BLK : (t - HEAD_TILES + 1) * BLK, :]

    def aggregate(src, i):
        blocks = [hidden[src, i * BLK : (i + 1) * BLK, :]]
        for k in range(1, NZB):
            j = pl.multiple_of(cols[i // 2, (i % 2) * NZB + k], BLK)
            blocks.append(hidden[src, pl.ds(j, BLK), :])
        lhs = jnp.concatenate([tile(i, k) for k in range(NZB)], axis=1)
        return (1.0 - ALPHA) * dot(lhs, jnp.concatenate(blocks, axis=0), ((1,), (0,)))

    chunks = start.shape[0] // (CHUNK * BLK)

    def pipeline(first, second, third):
        held = {}
        for s in range(chunks + 2):
            if s < chunks:
                first(s)
            if 0 <= s - 1 < chunks:
                held[s - 1] = second(s - 1)
            if 0 <= s - 2 < chunks:
                third(s - 2, held.pop(s - 2))

    def pick(values, l):
        out = jnp.float32(values[0])
        for n in range(1, len(values)):
            out = jnp.where(l == n, jnp.float32(values[n]), out)
        return out

    def rows_of(c):
        return slice(c * CHUNK * BLK, (c + 1) * CHUNK * BLK)

    def forward(l, _):
        src, dst = l % 2, (l + 1) % 2
        beta = pick(betas, l)
        w = weight[l]

        def first(c):
            for i in range(c * CHUNK, (c + 1) * CHUNK):
                rows = slice(i * BLK, (i + 1) * BLK)
                mixes[l, rows, :] = (aggregate(src, i) + start[rows, :]).astype(BF16)

        def second(c):
            return dot(mixes[l, rows_of(c), :], w, ((1,), (0,)))

        def third(c, product):
            rows = rows_of(c)
            pre = (1.0 - beta) * mixes[l, rows, :].astype(F32) + beta * product
            square = pre * pre
            t = jnp.tanh(pre * (GELU_C + (GELU_C * GELU_B) * square))
            half = 0.5 + 0.5 * t
            out = pre * half
            hidden[dst, rows, :] = out.astype(BF16)
            slopes[l, rows, :] = half + out * (1.0 - half) * (
                2.0 * GELU_C + (6.0 * GELU_C * GELU_B) * square
            )

        pipeline(first, second, third)
        return 0

    def backward(step, _, top=False):
        l = layers - 1 - step
        src, dst = step % 2, (step + 1) % 2
        beta = pick(betas, l)
        w = weight[l]

        def first(c):
            for i in range(c * CHUNK, (c + 1) * CHUNK):
                rows = slice(i * BLK, (i + 1) * BLK)
                if top:
                    back = cots[i // 2][(i % 2) * BLK : (i % 2 + 1) * BLK, :]
                else:
                    back = aggregate(src, i).astype(BF16)
                dpre[rows, :] = (slopes[l, rows, :] * back.astype(F32)).astype(BF16)

        def second(c):
            return dot(dpre[rows_of(c), :], w, ((1,), (1,)))

        def third(c, product):
            rows = rows_of(c)
            dmix = (1.0 - beta) * dpre[rows, :].astype(F32) + beta * product
            hidden[dst, rows, :] = dmix.astype(BF16)

        pipeline(first, second, third)
        term = ALPHA * hidden[dst, 0:256, :].astype(F32)
        grad_initial[0] = term if top else grad_initial[0] + term
        dw[...] = (beta * scale) * dot(mixes[l], dpre[...], ((0,), (0,)))
        grad_weights[l] = dw[pl.ds(pl.multiple_of(dom * 32, 32), 32), :]
        return 0

    lax.fori_loop(0, layers, forward, 0)
    backward(0, 0, top=True)
    lax.fori_loop(1, layers, backward, 0)
    for b in range(2):
        rows = slice(b * BLK, (b + 1) * BLK)
        back = aggregate(layers % 2, b).astype(BF16)
        grad_initial[0, rows, :] = grad_initial[0, rows, :] + back.astype(F32)


def run_layers(scale, betas, heads, tails, cots, weights):
    vmem = pl.BlockSpec(memory_space=pltpu.VMEM)
    nodes, width = 2048, 256
    return pl.pallas_call(
        functools.partial(layers_kernel, scale, betas),
        in_specs=[vmem] * 28,
        out_specs=[vmem, vmem],
        out_shape=[
            jax.ShapeDtypeStruct((1, 256, width), F32),
            jax.ShapeDtypeStruct((4, 32, width), F32),
        ],
        scratch_shapes=[
            pltpu.VMEM((nodes, width), F32),
            pltpu.VMEM((4, width, width), BF16),
            pltpu.VMEM((8, BLK), jnp.int32),
            pltpu.SMEM((8, BLK), jnp.int32),
            pltpu.VMEM((2, nodes, width), BF16),
            pltpu.VMEM((4, nodes, width), BF16),
            pltpu.VMEM((4, nodes, width), F32),
            pltpu.VMEM((nodes, width), BF16),
            pltpu.VMEM((width, width), F32),
            pltpu.SemaphoreType.DMA,
        ],
        compiler_params=pltpu.CompilerParams(vmem_limit_bytes=40 * 1024 * 1024),
        cost_estimate=pl.CostEstimate(flops=9_000_000_000, bytes_accessed=6_000_000, transcendentals=0),
        name="layers",
    )(*heads, *tails, *cots, *weights)


def ring(v, step):
    return lax.ppermute(v, "dom", [(i, (i + 2 * step) % 8) for i in range(8)])


def other_core(v):
    return lax.ppermute(v, "dom", [(i, i ^ 1) for i in range(8)])


def both_cores(pieces):
    out = []
    for piece in pieces:
        out += [piece, other_core(piece)]
    return out


def local(initial, block_cols, block_tiles, layer_weights, cotangent):
    layers = lax.axis_size("phase")
    nodes_all = 4 * 2048 * lax.axis_size("dp")
    scale = 1.0 / math.sqrt(nodes_all)
    betas = [math.log(THETA / (l + 1) + 1.0) for l in range(layers)]
    spans, rows = block_tiles.shape[:2]
    tiles = block_tiles.reshape(spans, rows * NZB, BLK, BLK)
    head, tail, cot = pack(tiles, initial, cotangent, block_cols)
    head_left, head_right = ring(head, 1), ring(head, -1)
    tail_left, tail_right = ring(tail, 1), ring(tail, -1)
    heads = both_cores([head, head_left, ring(head_left, 1), head_right])
    tails = both_cores([tail, tail_left, ring(tail_right, -1), tail_right])
    weights = [layer_weights] + [
        lax.ppermute(layer_weights, "phase", [(i, (i + n) % 4) for i in range(4)]) for n in (1, 2, 3)
    ]
    cot, head_left, tail_right = lax.optimization_barrier((cot, head_left, tail_right))
    cot_left, cot_right = ring(cot, 1), ring(cot, -1)
    cots = both_cores([cot, cot_left, ring(cot_left, 1), cot_right])
    grad_initial, parts = run_layers(scale, betas, heads, tails, cots, weights)
    parts = lax.all_to_all(parts, "phase", 0, 0, tiled=True)
    mine = jnp.sum(parts, axis=0)
    mine = jnp.broadcast_to(mine[None], (8,) + mine.shape)
    mine = jnp.sum(lax.all_to_all(mine, "dp", 0, 0, tiled=True), axis=0)
    mine = jnp.broadcast_to(mine[None], (8,) + mine.shape)
    mine = lax.all_to_all(mine, "dom", 0, 0, tiled=True)
    return grad_initial, mine.reshape(1, 256, 256)


def solution(mesh):
    placed = (
        P("dp", "dom", None),
        P("dp", "dom", None),
        P("dp", "dom", None, None, None),
        P("phase", None, None),
        P("dp", "dom", None),
    )
    return jax.shard_map(
        local,
        mesh=mesh,
        in_specs=placed,
        out_specs=(P(("dp", "phase"), "dom", None), P("phase", None, None)),
        check_vma=False,
    )
```

```python
import functools
import math

import jax
import jax.numpy as jnp
from jax import lax
from jax.experimental import pallas as pl
from jax.experimental.pallas import tpu as pltpu
from jax.sharding import PartitionSpec as P

ALPHA = 0.1
THETA = 0.5
BLK = 128
NZB = 5
GELU_C = math.sqrt(2.0 / math.pi)
GELU_B = 0.044715
ROWS = 2 * BLK
TILE_ROWS = 2 * NZB * BLK
CUT = 9 * BLK
START = TILE_ROWS
COT = START + 2 * ROWS
COLS = COT + 2 * ROWS
PIECE = COLS + 16
CHUNK = 4
LAG = 8
GELU_C = math.sqrt(2.0 / math.pi)
GELU_B = 0.044715
HEAD_TILES = 7
TAIL_START = (2 * NZB - HEAD_TILES) * BLK
TAIL_COLS = TAIL_START + 512
CHUNK = 4
LAG = 8
BF16 = jnp.bfloat16
F32 = jnp.float32


def pack_kernel(tiles, initial, cotangent, cols, piece, start, cot, sems):
    span = lax.axis_index("phase")
    copies = [(initial.at[span], start), (cotangent.at[span], cot)]
    for t in range(2 * NZB):
        copies.append((tiles.at[span, t], piece.at[pl.ds(t * BLK, BLK)]))
    started = [pltpu.make_async_copy(a, b, sems.at[n]) for n, (a, b) in enumerate(copies)]
    for c in started:
        c.start()
    lane = lax.broadcasted_iota(jnp.int32, (16, BLK), 1)
    vec = jnp.zeros((16, BLK), F32)
    for b in range(2):
        for k in range(NZB):
            vec = jnp.where(lane == b * NZB + k, cols[span, b, k].astype(F32), vec)
    piece[COLS : COLS + 16, :] = vec.astype(BF16)
    for c in started:
        c.wait()
    for base, array in ((START, start), (COT, cot)):
        piece[base : base + ROWS, :] = array[:, :BLK]
        piece[base + ROWS : base + 2 * ROWS, :] = array[:, BLK:]


def pack(tiles, initial, cotangent, cols):
    any_spec = pl.BlockSpec(memory_space=pl.ANY)
    return pl.pallas_call(
        pack_kernel,
        in_specs=[any_spec, any_spec, any_spec, pl.BlockSpec(memory_space=pltpu.SMEM)],
        out_specs=pl.BlockSpec(memory_space=pltpu.VMEM),
        out_shape=pltpu.VMEM((PIECE, BLK), BF16),
        scratch_shapes=[
            pltpu.VMEM((ROWS, 2 * BLK), BF16),
            pltpu.VMEM((ROWS, 2 * BLK), BF16),
            pltpu.SemaphoreType.DMA((2 + 2 * NZB,)),
        ],
        name="pack",
    )(*[pltpu.with_memory_space_constraint(a, pltpu.HBM) for a in (tiles, initial, cotangent)], cols)


def dot(a, b, dims):
    return lax.dot_general(a, b, (dims, ((), ())), preferred_element_type=F32)


def layers_kernel(scale, betas, layout, *refs):
    count = sum(len(p) for p in layout)
    inputs, weights = list(refs[:count]), refs[count : count + len(betas)]
    grad_initial, grad_weights = refs[count + len(betas) : count + len(betas) + 2]
    scratch = refs[count + len(betas) + 2 :]
    start, weight, cols_int, cols, hidden, mixes, slopes, dpre, dw, sem = scratch
    pieces = []
    for parts in layout:
        spots = []
        for low, high in parts:
            spots.append((low, high, inputs.pop(0)))
        pieces.append(spots)

    def piece(n, low, rows):
        for first, last, ref in pieces[n]:
            if first <= low < last:
                return ref[low - first : low - first + rows, :]

    dom = lax.axis_index("dom")
    phase = lax.axis_index("phase")
    x, core = dom // 2, dom % 2
    layers = len(weights)
    for n in range(layers):
        weight[(phase - n + layers) % layers] = weights[n][0]
    for n in range(8):
        j = piece(n, COLS, 16).astype(F32).astype(jnp.int32)
        chip = lax.bitwise_and(x - lax.shift_right_logical(j, 2) + 4, 3)
        side = lax.bitwise_xor(lax.bitwise_and(lax.shift_right_logical(j, 1), 1), core)
        place = chip * 4 + side * 2 + lax.bitwise_and(j, 1)
        cols_int[n : n + 1, :] = (place * BLK)[:1]
    to_scalars = pltpu.make_async_copy(cols_int, cols, sem)
    to_scalars.start()
    for n in range(8):
        for half in range(2):
            part = piece(n, START + ROWS * half, ROWS)
            lanes = slice(BLK * half, BLK * (half + 1))
            hidden[0, ROWS * n : ROWS * (n + 1), lanes] = part
            start[ROWS * n : ROWS * (n + 1), lanes] = ALPHA * part.astype(F32)
    to_scalars.wait()

    def tile(i, k):
        return piece(i // 2, ((i % 2) * NZB + k) * BLK, BLK)

    def aggregate(src, i):
        blocks = [hidden[src, i * BLK : (i + 1) * BLK, :]]
        for k in range(1, NZB):
            j = pl.multiple_of(cols[i // 2, (i % 2) * NZB + k], BLK)
            blocks.append(hidden[src, pl.ds(j, BLK), :])
        lhs = jnp.concatenate([tile(i, k) for k in range(NZB)], axis=1)
        return (1.0 - ALPHA) * dot(lhs, jnp.concatenate(blocks, axis=0), ((1,), (0,)))

    blocks_all = start.shape[0] // BLK

    def pipeline(first, second, third):
        held = {}
        for s in range(blocks_all + LAG):
            if s < blocks_all:
                first(s)
            if s < blocks_all + CHUNK and s >= CHUNK and s % CHUNK == 0:
                held[s // CHUNK - 1] = second(s // CHUNK - 1)
            i = s - LAG
            if 0 <= i < blocks_all:
                product = held[i // CHUNK]
                third(i, product[(i % CHUNK) * BLK : (i % CHUNK + 1) * BLK, :])

    def pick(values, l):
        out = jnp.float32(values[0])
        for n in range(1, len(values)):
            out = jnp.where(l == n, jnp.float32(values[n]), out)
        return out

    def forward(l, _):
        src, dst = l % 2, (l + 1) % 2
        beta = pick(betas, l)
        w = weight[l]

        def first(i):
            rows = slice(i * BLK, (i + 1) * BLK)
            mixes[l, rows, :] = (aggregate(src, i) + start[rows, :]).astype(BF16)

        def second(c):
            return dot(mixes[l, c * CHUNK * BLK : (c + 1) * CHUNK * BLK, :], w, ((1,), (0,)))

        def third(i, product):
            rows = slice(i * BLK, (i + 1) * BLK)
            pre = (1.0 - beta) * mixes[l, rows, :].astype(F32) + beta * product
            square = pre * pre
            t = jnp.tanh(pre * (GELU_C + (GELU_C * GELU_B) * square))
            half = 0.5 + 0.5 * t
            out = pre * half
            hidden[dst, rows, :] = out.astype(BF16)
            slopes[l, rows, :] = half + out * (1.0 - half) * (
                2.0 * GELU_C + (6.0 * GELU_C * GELU_B) * square
            )

        pipeline(first, second, third)
        return 0

    def backward(step, _, top=False):
        l = layers - 1 - step
        src, dst = step % 2, (step + 1) % 2
        beta = pick(betas, l)
        w = weight[l]

        def first(i):
            rows = slice(i * BLK, (i + 1) * BLK)
            if top:
                low = COT + (i % 2) * BLK
                back = jnp.concatenate([piece(i // 2, low, BLK), piece(i // 2, low + ROWS, BLK)], axis=1)
            else:
                back = aggregate(src, i).astype(BF16)
            dpre[rows, :] = (slopes[l, rows, :] * back.astype(F32)).astype(BF16)

        def second(c):
            return dot(dpre[c * CHUNK * BLK : (c + 1) * CHUNK * BLK, :], w, ((1,), (1,)))

        def third(i, product):
            rows = slice(i * BLK, (i + 1) * BLK)
            dmix = (1.0 - beta) * dpre[rows, :].astype(F32) + beta * product
            hidden[dst, rows, :] = dmix.astype(BF16)

        pipeline(first, second, third)
        term = ALPHA * hidden[dst, 0:256, :].astype(F32)
        grad_initial[0] = term if top else grad_initial[0] + term
        lanes = pl.ds(pl.multiple_of(dom // 4 * BLK, BLK), BLK)
        dw[...] = (beta * scale) * dot(mixes[l, :, lanes], dpre[...], ((0,), (0,)))
        grad_weights[l] = dw[pl.ds(pl.multiple_of(dom % 4 * 32, 32), 32), :].astype(BF16)
        return 0

    lax.fori_loop(0, layers, forward, 0)
    backward(0, 0, top=True)
    lax.fori_loop(1, layers, backward, 0)
    for b in range(2):
        rows = slice(b * BLK, (b + 1) * BLK)
        back = aggregate(layers % 2, b).astype(BF16)
        grad_initial[0, rows, :] = grad_initial[0, rows, :] + back.astype(F32)


def run_layers(scale, betas, pieces, weights):
    vmem = pl.BlockSpec(memory_space=pltpu.VMEM)
    layout = [[(low, high) for low, high, _ in parts] for parts in pieces]
    arrays = [a for parts in pieces for _, _, a in parts]
    nodes, width = 2048, 256
    return pl.pallas_call(
        functools.partial(layers_kernel, scale, betas, layout),
        in_specs=[vmem] * (len(arrays) + len(weights)),
        out_specs=[vmem, vmem],
        out_shape=[
            jax.ShapeDtypeStruct((1, 256, width), F32),
            jax.ShapeDtypeStruct((4, 32, width), BF16),
        ],
        scratch_shapes=[
            pltpu.VMEM((nodes, width), F32),
            pltpu.VMEM((4, width, width), BF16),
            pltpu.VMEM((8, BLK), jnp.int32),
            pltpu.SMEM((8, BLK), jnp.int32),
            pltpu.VMEM((2, nodes, width), BF16),
            pltpu.VMEM((4, nodes, width), BF16),
            pltpu.VMEM((4, nodes, width), F32),
            pltpu.VMEM((nodes, width), BF16),
            pltpu.VMEM((BLK, width), F32),
            pltpu.SemaphoreType.DMA,
        ],
        compiler_params=pltpu.CompilerParams(vmem_limit_bytes=40 * 1024 * 1024),
        cost_estimate=pl.CostEstimate(flops=9_000_000_000, bytes_accessed=6_000_000, transcendentals=0),
        name="layers",
    )(*arrays, *weights)


def ring(v, step):
    return lax.ppermute(v, "dom", [(i, (i + 2 * step) % 8) for i in range(8)])


def other_core(v):
    return lax.ppermute(v, "dom", [(i, i ^ 1) for i in range(8)])


def phase_weights(w):
    return [w] + [lax.ppermute(w, "phase", [(i, (i + n) % 4) for i in range(4)]) for n in (1, 2, 3)]


def whole(v):
    return [(0, PIECE, v)]


def gather_halves(own, w):
    left, right = ring(own, 1), ring(own, -1)
    w, _ = lax.optimization_barrier((w, own))
    weights = phase_weights(w)
    top, low = ring(left[:CUT], 1), ring(right[CUT:], -1)
    pieces = [whole(own), whole(other_core(own)), whole(left), whole(other_core(left))]
    pieces.append([(0, CUT, top), (CUT, PIECE, low)])
    pieces.append([(0, CUT, other_core(top)), (CUT, PIECE, other_core(low))])
    pieces += [whole(right), whole(other_core(right))]
    return pieces, weights


def local(initial, block_cols, block_tiles, layer_weights, cotangent):
    layers = lax.axis_size("phase")
    nodes_all = 4 * 2048 * lax.axis_size("dp")
    scale = 1.0 / math.sqrt(nodes_all)
    betas = [math.log(THETA / (l + 1) + 1.0) for l in range(layers)]
    spans, rows = block_tiles.shape[:2]
    tiles = block_tiles.reshape(spans, rows * NZB, BLK, BLK)
    own = pack(tiles, initial, cotangent, block_cols)
    pieces, weights = gather_halves(own, layer_weights)
    grad_initial, parts = run_layers(scale, betas, pieces, weights)
    parts = lax.all_to_all(parts, "phase", 0, 0, tiled=True)
    mine = jnp.sum(parts.astype(F32), axis=0).astype(BF16)
    mine = jnp.broadcast_to(mine[None], (8,) + mine.shape)
    mine = jnp.sum(lax.all_to_all(mine, "dp", 0, 0, tiled=True).astype(F32), axis=0)
    mine = jnp.broadcast_to(mine[None], (8,) + mine.shape)
    mine = lax.all_to_all(mine, "dom", 0, 0, tiled=True)
    return grad_initial, mine.reshape(1, 256, 256)


def solution(mesh):
    placed = (
        P("dp", "dom", None),
        P("dp", "dom", None),
        P("dp", "dom", None, None, None),
        P("phase", None, None),
        P("dp", "dom", None),
    )
    return jax.shard_map(
        local,
        mesh=mesh,
        in_specs=placed,
        out_specs=(P(("dp", "phase"), "dom", None), P("phase", None, None)),
        check_vma=False,
    )
```

```python
import functools
import math

import jax
import jax.numpy as jnp
from jax import lax
from jax.experimental import pallas as pl
from jax.experimental.pallas import tpu as pltpu
from jax.sharding import PartitionSpec as P

ALPHA = 0.1
THETA = 0.5
BLK = 128
NZB = 5
GELU_C = math.sqrt(2.0 / math.pi)
GELU_B = 0.044715
ROWS = 2 * BLK
TILE_ROWS = 2 * NZB * BLK
START = TILE_ROWS
COT = START + 2 * ROWS
COLS = COT + 2 * ROWS
PIECE = COLS + 16
CHUNK = 4
LAG = 8
GELU_C = math.sqrt(2.0 / math.pi)
GELU_B = 0.044715
HEAD_TILES = 7
TAIL_START = (2 * NZB - HEAD_TILES) * BLK
TAIL_COLS = TAIL_START + 512
CHUNK = 4
LAG = 8
BF16 = jnp.bfloat16
F32 = jnp.float32


def pack_kernel(tiles, initial, cotangent, cols, piece, start, cot, sems):
    span = lax.axis_index("phase")
    copies = [(initial.at[span], start), (cotangent.at[span], cot)]
    for t in range(2 * NZB):
        copies.append((tiles.at[span, t], piece.at[pl.ds(t * BLK, BLK)]))
    started = [pltpu.make_async_copy(a, b, sems.at[n]) for n, (a, b) in enumerate(copies)]
    for c in started:
        c.start()
    lane = lax.broadcasted_iota(jnp.int32, (16, BLK), 1)
    vec = jnp.zeros((16, BLK), F32)
    for b in range(2):
        for k in range(NZB):
            vec = jnp.where(lane == b * NZB + k, cols[span, b, k].astype(F32), vec)
    piece[COLS : COLS + 16, :] = vec.astype(BF16)
    for c in started:
        c.wait()
    for base, array in ((START, start), (COT, cot)):
        piece[base : base + ROWS, :] = array[:, :BLK]
        piece[base + ROWS : base + 2 * ROWS, :] = array[:, BLK:]


def pack(tiles, initial, cotangent, cols):
    any_spec = pl.BlockSpec(memory_space=pl.ANY)
    return pl.pallas_call(
        pack_kernel,
        in_specs=[any_spec, any_spec, any_spec, pl.BlockSpec(memory_space=pltpu.SMEM)],
        out_specs=pl.BlockSpec(memory_space=pltpu.VMEM),
        out_shape=pltpu.VMEM((PIECE, BLK), BF16),
        scratch_shapes=[
            pltpu.VMEM((ROWS, 2 * BLK), BF16),
            pltpu.VMEM((ROWS, 2 * BLK), BF16),
            pltpu.SemaphoreType.DMA((2 + 2 * NZB,)),
        ],
        name="pack",
    )(*[pltpu.with_memory_space_constraint(a, pltpu.HBM) for a in (tiles, initial, cotangent)], cols)


def dot(a, b, dims):
    return lax.dot_general(a, b, (dims, ((), ())), preferred_element_type=F32)


def layers_kernel(scale, betas, *refs):
    layers = len(betas)
    pieces, weights = refs[:8], refs[8 : 8 + layers]
    grad_initial, grad_weights = refs[8 + layers : 10 + layers]
    start, weight, cols_int, cols, hidden, mixes, slopes, dpre, dw, sem = refs[10 + layers :]

    def piece(n, low, rows):
        return pieces[n][low : low + rows, :]

    dom = lax.axis_index("dom")
    phase = lax.axis_index("phase")
    x, core = dom // 2, dom % 2
    for n in range(layers):
        weight[(phase - n + layers) % layers] = weights[n][0]
    way = 1 - 2 * core
    for n in range(8):
        j = piece(n, COLS, 16).astype(F32).astype(jnp.int32)
        chip = lax.bitwise_and(way * (x - lax.shift_right_logical(j, 2)) + 4, 3)
        side = lax.bitwise_xor(lax.bitwise_and(lax.shift_right_logical(j, 1), 1), core)
        place = chip * 4 + side * 2 + lax.bitwise_and(j, 1)
        cols_int[n : n + 1, :] = (place * BLK)[:1]
    to_scalars = pltpu.make_async_copy(cols_int, cols, sem)
    to_scalars.start()
    for n in range(8):
        for half in range(2):
            part = piece(n, START + ROWS * half, ROWS)
            lanes = slice(BLK * half, BLK * (half + 1))
            hidden[0, ROWS * n : ROWS * (n + 1), lanes] = part
            start[ROWS * n : ROWS * (n + 1), lanes] = ALPHA * part.astype(F32)
    to_scalars.wait()

    def tile(i, k):
        return piece(i // 2, ((i % 2) * NZB + k) * BLK, BLK)

    def aggregate(src, i):
        blocks = [hidden[src, i * BLK : (i + 1) * BLK, :]]
        for k in range(1, NZB):
            j = pl.multiple_of(cols[i // 2, (i % 2) * NZB + k], BLK)
            blocks.append(hidden[src, pl.ds(j, BLK), :])
        lhs = jnp.concatenate([tile(i, k) for k in range(NZB)], axis=1)
        return (1.0 - ALPHA) * dot(lhs, jnp.concatenate(blocks, axis=0), ((1,), (0,)))

    blocks_all = start.shape[0] // BLK

    def pipeline(first, second, third):
        held = {}
        for s in range(blocks_all + LAG):
            if s < blocks_all:
                first(s)
            if s < blocks_all + CHUNK and s >= CHUNK and s % CHUNK == 0:
                held[s // CHUNK - 1] = second(s // CHUNK - 1)
            i = s - LAG
            if 0 <= i < blocks_all:
                product = held[i // CHUNK]
                third(i, product[(i % CHUNK) * BLK : (i % CHUNK + 1) * BLK, :])

    def pick(values, l):
        out = jnp.float32(values[0])
        for n in range(1, len(values)):
            out = jnp.where(l == n, jnp.float32(values[n]), out)
        return out

    def forward(l, _):
        src, dst = l % 2, (l + 1) % 2
        beta = pick(betas, l)
        w = weight[l]

        def first(i):
            rows = slice(i * BLK, (i + 1) * BLK)
            mixes[l, rows, :] = (aggregate(src, i) + start[rows, :]).astype(BF16)

        def second(c):
            return dot(mixes[l, c * CHUNK * BLK : (c + 1) * CHUNK * BLK, :], w, ((1,), (0,)))

        def third(i, product):
            rows = slice(i * BLK, (i + 1) * BLK)
            pre = (1.0 - beta) * mixes[l, rows, :].astype(F32) + beta * product
            square = pre * pre
            t = jnp.tanh(pre * (GELU_C + (GELU_C * GELU_B) * square))
            half = 0.5 + 0.5 * t
            out = pre * half
            hidden[dst, rows, :] = out.astype(BF16)
            slopes[l, rows, :] = half + out * (1.0 - half) * (
                2.0 * GELU_C + (6.0 * GELU_C * GELU_B) * square
            )

        pipeline(first, second, third)
        return 0

    def backward(step, _, top=False):
        l = layers - 1 - step
        src, dst = step % 2, (step + 1) % 2
        beta = pick(betas, l)
        w = weight[l]

        def first(i):
            rows = slice(i * BLK, (i + 1) * BLK)
            if top:
                low = COT + (i % 2) * BLK
                back = jnp.concatenate([piece(i // 2, low, BLK), piece(i // 2, low + ROWS, BLK)], axis=1)
            else:
                back = aggregate(src, i).astype(BF16)
            dpre[rows, :] = (slopes[l, rows, :] * back.astype(F32)).astype(BF16)

        def second(c):
            return dot(dpre[c * CHUNK * BLK : (c + 1) * CHUNK * BLK, :], w, ((1,), (1,)))

        def third(i, product):
            rows = slice(i * BLK, (i + 1) * BLK)
            dmix = (1.0 - beta) * dpre[rows, :].astype(F32) + beta * product
            hidden[dst, rows, :] = dmix.astype(BF16)

        pipeline(first, second, third)
        term = ALPHA * hidden[dst, 0:256, :].astype(F32)
        grad_initial[0] = term if top else grad_initial[0] + term
        lanes = pl.ds(pl.multiple_of(dom // 4 * BLK, BLK), BLK)
        dw[...] = (beta * scale) * dot(mixes[l, :, lanes], dpre[...], ((0,), (0,)))
        grad_weights[l] = dw[pl.ds(pl.multiple_of(dom % 4 * 32, 32), 32), :].astype(BF16)
        return 0

    lax.fori_loop(0, layers, forward, 0)
    backward(0, 0, top=True)
    lax.fori_loop(1, layers, backward, 0)
    for b in range(2):
        rows = slice(b * BLK, (b + 1) * BLK)
        back = aggregate(layers % 2, b).astype(BF16)
        grad_initial[0, rows, :] = grad_initial[0, rows, :] + back.astype(F32)


def run_layers(scale, betas, pieces, weights):
    vmem = pl.BlockSpec(memory_space=pltpu.VMEM)
    nodes, width = 2048, 256
    return pl.pallas_call(
        functools.partial(layers_kernel, scale, betas),
        in_specs=[vmem] * (len(pieces) + len(weights)),
        out_specs=[vmem, vmem],
        out_shape=[
            jax.ShapeDtypeStruct((1, 256, width), F32),
            jax.ShapeDtypeStruct((4, 32, width), BF16),
        ],
        scratch_shapes=[
            pltpu.VMEM((nodes, width), F32),
            pltpu.VMEM((4, width, width), BF16),
            pltpu.VMEM((8, BLK), jnp.int32),
            pltpu.SMEM((8, BLK), jnp.int32),
            pltpu.VMEM((2, nodes, width), BF16),
            pltpu.VMEM((4, nodes, width), BF16),
            pltpu.VMEM((4, nodes, width), F32),
            pltpu.VMEM((nodes, width), BF16),
            pltpu.VMEM((BLK, width), F32),
            pltpu.SemaphoreType.DMA,
        ],
        compiler_params=pltpu.CompilerParams(vmem_limit_bytes=40 * 1024 * 1024),
        cost_estimate=pl.CostEstimate(flops=9_000_000_000, bytes_accessed=6_000_000, transcendentals=0),
        name="layers",
    )(*pieces, *weights)


def onward(v):
    route = [(i, (i + 2) % 8 if i % 2 == 0 else (i - 2) % 8) for i in range(8)]
    return lax.ppermute(v, "dom", route)


def other_core(v):
    return lax.ppermute(v, "dom", [(i, i ^ 1) for i in range(8)])


def phase_weights(w):
    return [w] + [lax.ppermute(w, "phase", [(i, (i + n) % 4) for i in range(4)]) for n in (1, 2, 3)]


def across(v):
    route = [(i, (i + 2) % 8 - 1 if i % 2 else (i - 2) % 8 + 1) for i in range(8)]
    return lax.ppermute(v, "dom", route)


def gather(own, w):
    near, near_too = onward(own), across(own)
    partner = other_core(own)
    weights = phase_weights(w)
    early, *weights = lax.optimization_barrier((near, *weights))
    far = onward(early)
    pieces = [own, partner, near, near_too, far, other_core(far), other_core(near_too), other_core(near)]
    return pieces, weights


def local(initial, block_cols, block_tiles, layer_weights, cotangent):
    layers = lax.axis_size("phase")
    nodes_all = 4 * 2048 * lax.axis_size("dp")
    scale = 1.0 / math.sqrt(nodes_all)
    betas = [math.log(THETA / (l + 1) + 1.0) for l in range(layers)]
    spans, rows = block_tiles.shape[:2]
    tiles = block_tiles.reshape(spans, rows * NZB, BLK, BLK)
    own = pack(tiles, initial, cotangent, block_cols)
    pieces, weights = gather(own, layer_weights)
    grad_initial, parts = run_layers(scale, betas, pieces, weights)
    parts = lax.all_to_all(parts, "phase", 0, 0, tiled=True)
    mine = jnp.sum(parts.astype(F32), axis=0).astype(BF16)
    mine = jnp.broadcast_to(mine[None], (8,) + mine.shape)
    mine = jnp.sum(lax.all_to_all(mine, "dp", 0, 0, tiled=True).astype(F32), axis=0)
    mine = jnp.broadcast_to(mine[None], (8,) + mine.shape)
    mine = lax.all_to_all(mine, "dom", 0, 0, tiled=True)
    return grad_initial, mine.reshape(1, 256, 256)


def solution(mesh):
    placed = (
        P("dp", "dom", None),
        P("dp", "dom", None),
        P("dp", "dom", None, None, None),
        P("phase", None, None),
        P("dp", "dom", None),
    )
    return jax.shard_map(
        local,
        mesh=mesh,
        in_specs=placed,
        out_specs=(P(("dp", "phase"), "dom", None), P("phase", None, None)),
        check_vma=False,
    )
```

```python
import functools
import math

import jax
import jax.numpy as jnp
from jax import lax
from jax.experimental import pallas as pl
from jax.experimental.pallas import tpu as pltpu
from jax.sharding import PartitionSpec as P

ALPHA = 0.1
THETA = 0.5
BLK = 128
NZB = 5
GELU_C = math.sqrt(2.0 / math.pi)
GELU_B = 0.044715
ROWS = 2 * BLK
TILE_ROWS = 2 * NZB * BLK
START = TILE_ROWS
COT = START + 2 * ROWS
COLS = COT + 2 * ROWS
PIECE = COLS + 16
CHUNK = 4
LAG = 8
GELU_C = math.sqrt(2.0 / math.pi)
GELU_B = 0.044715
HEAD_TILES = 7
TAIL_START = (2 * NZB - HEAD_TILES) * BLK
TAIL_COLS = TAIL_START + 512
CHUNK = 4
LAG = 8
BF16 = jnp.bfloat16
F32 = jnp.float32


def pack_kernel(tiles, initial, cotangent, cols, piece, start, cot, sems):
    span = lax.axis_index("phase")
    copies = [
        (initial.at[span], start),
        (cotangent.at[span], cot),
        (tiles.at[span], piece.at[pl.ds(0, TILE_ROWS)]),
    ]
    started = [pltpu.make_async_copy(a, b, sems.at[n]) for n, (a, b) in enumerate(copies)]
    for c in started:
        c.start()
    lane = lax.broadcasted_iota(jnp.int32, (16, BLK), 1)
    vec = jnp.zeros((16, BLK), F32)
    for b in range(2):
        for k in range(NZB):
            vec = jnp.where(lane == b * NZB + k, cols[span, b, k].astype(F32), vec)
    piece[COLS : COLS + 16, :] = vec.astype(BF16)
    for copy, base, array in ((started[0], START, start), (started[1], COT, cot)):
        copy.wait()
        piece[base : base + ROWS, :] = array[:, :BLK]
        piece[base + ROWS : base + 2 * ROWS, :] = array[:, BLK:]
    started[2].wait()


def pack(tiles, initial, cotangent, cols):
    any_spec = pl.BlockSpec(memory_space=pl.ANY)
    return pl.pallas_call(
        pack_kernel,
        in_specs=[any_spec, any_spec, any_spec, pl.BlockSpec(memory_space=pltpu.SMEM)],
        out_specs=pl.BlockSpec(memory_space=pltpu.VMEM),
        out_shape=pltpu.VMEM((PIECE, BLK), BF16),
        scratch_shapes=[
            pltpu.VMEM((ROWS, 2 * BLK), BF16),
            pltpu.VMEM((ROWS, 2 * BLK), BF16),
            pltpu.SemaphoreType.DMA((3,)),
        ],
        name="pack",
    )(*[pltpu.with_memory_space_constraint(a, pltpu.HBM) for a in (tiles, initial, cotangent)], cols)


def dot(a, b, dims):
    return lax.dot_general(a, b, (dims, ((), ())), preferred_element_type=F32)


def layers_kernel(scale, betas, *refs):
    layers = len(betas)
    pieces, weights = refs[:8], refs[8 : 8 + layers]
    grad_initial, grad_weights = refs[8 + layers : 10 + layers]
    start, weight, cols_int, cols, h_even, h_odd, mixes, slopes, dpre, dw, sem = refs[10 + layers :]

    hidden = (h_even, h_odd)

    def piece(n, low, rows):
        return pieces[n][low : low + rows, :]

    dom = lax.axis_index("dom")
    phase = lax.axis_index("phase")
    x, core = dom // 2, dom % 2
    for n in range(layers):
        weight[(phase - n + layers) % layers] = weights[n][0]
    way = 1 - 2 * core
    for n in range(8):
        j = piece(n, COLS, 16).astype(F32).astype(jnp.int32)
        chip = lax.bitwise_and(way * (x - lax.shift_right_logical(j, 2)) + 4, 3)
        side = lax.bitwise_xor(lax.bitwise_and(lax.shift_right_logical(j, 1), 1), core)
        place = chip * 4 + side * 2 + lax.bitwise_and(j, 1)
        cols_int[n : n + 1, :] = (place * BLK)[:1]
    to_scalars = pltpu.make_async_copy(cols_int, cols, sem)
    to_scalars.start()
    for n in range(8):
        for half in range(2):
            part = piece(n, START + ROWS * half, ROWS)
            lanes = slice(BLK * half, BLK * (half + 1))
            h_even[ROWS * n : ROWS * (n + 1), lanes] = part
            start[ROWS * n : ROWS * (n + 1), lanes] = ALPHA * part.astype(F32)
    to_scalars.wait()

    def tile(i, k):
        return piece(i // 2, ((i % 2) * NZB + k) * BLK, BLK)

    def aggregate(src, i):
        blocks = [hidden[src][i * BLK : (i + 1) * BLK, :]]
        for k in range(1, NZB):
            j = pl.multiple_of(cols[i // 2, (i % 2) * NZB + k], BLK)
            blocks.append(hidden[src][pl.ds(j, BLK), :])
        lhs = jnp.concatenate([tile(i, k) for k in range(NZB)], axis=1)
        return (1.0 - ALPHA) * dot(lhs, jnp.concatenate(blocks, axis=0), ((1,), (0,)))

    blocks_all = start.shape[0] // BLK

    def pipeline(first, second, third):
        held = {}
        for s in range(blocks_all + LAG):
            if s < blocks_all:
                first(s)
            if s < blocks_all + CHUNK and s >= CHUNK and s % CHUNK == 0:
                held[s // CHUNK - 1] = second(s // CHUNK - 1)
            i = s - LAG
            if 0 <= i < blocks_all:
                product = held[i // CHUNK]
                third(i, product[(i % CHUNK) * BLK : (i % CHUNK + 1) * BLK, :])

    def pick(values, l):
        if isinstance(l, int):
            return values[l]
        out = jnp.float32(values[0])
        for n in range(1, len(values)):
            out = jnp.where(l == n, jnp.float32(values[n]), out)
        return out

    def forward(l, src):
        dst = 1 - src
        beta = pick(betas, l)
        w = weight[l]

        def first(i):
            rows = slice(i * BLK, (i + 1) * BLK)
            mixes[l, rows, :] = (aggregate(src, i) + start[rows, :]).astype(BF16)

        def second(c):
            return dot(mixes[l, c * CHUNK * BLK : (c + 1) * CHUNK * BLK, :], w, ((1,), (0,)))

        def third(i, product):
            rows = slice(i * BLK, (i + 1) * BLK)
            pre = (1.0 - beta) * mixes[l, rows, :].astype(F32) + beta * product
            square = pre * pre
            t = jnp.tanh(pre * (GELU_C + (GELU_C * GELU_B) * square))
            half = 0.5 + 0.5 * t
            out = pre * half
            hidden[dst][rows, :] = out.astype(BF16)
            slopes[l, rows, :] = half + out * (1.0 - half) * (
                2.0 * GELU_C + (6.0 * GELU_C * GELU_B) * square
            )

        pipeline(first, second, third)
        return 0

    def backward(step, src, top=False):
        l = layers - 1 - step
        dst = 1 - src
        beta = pick(betas, l)
        w = weight[l]

        def first(i):
            rows = slice(i * BLK, (i + 1) * BLK)
            if top:
                low = COT + (i % 2) * BLK
                back = jnp.concatenate([piece(i // 2, low, BLK), piece(i // 2, low + ROWS, BLK)], axis=1)
            else:
                back = aggregate(src, i).astype(BF16)
            dpre[rows, :] = (slopes[l, rows, :] * back.astype(F32)).astype(BF16)

        def second(c):
            return dot(dpre[c * CHUNK * BLK : (c + 1) * CHUNK * BLK, :], w, ((1,), (1,)))

        def third(i, product):
            rows = slice(i * BLK, (i + 1) * BLK)
            dmix = (1.0 - beta) * dpre[rows, :].astype(F32) + beta * product
            hidden[dst][rows, :] = dmix.astype(BF16)

        pipeline(first, second, third)
        term = ALPHA * hidden[dst][0:256, :].astype(F32)
        grad_initial[0] = term if top else grad_initial[0] + term
        lanes = pl.ds(pl.multiple_of(core * BLK, BLK), BLK)
        dw[...] = (beta * scale) * dot(mixes[l, :, lanes], dpre[...], ((0,), (0,)))
        grad_weights[l] = dw[pl.ds(pl.multiple_of(x % 2 * 64, 64), 64), :].astype(BF16)
        return 0

    def two_forward(m, _):
        forward(2 * m, 0)
        forward(2 * m + 1, 1)
        return 0

    def two_backward(m, _):
        backward(2 * m, 0)
        backward(2 * m + 1, 1)
        return 0

    lax.fori_loop(0, layers // 2, two_forward, 0)
    backward(0, 0, top=True)
    backward(1, 1)
    lax.fori_loop(1, layers // 2, two_backward, 0)
    for b in range(2):
        rows = slice(b * BLK, (b + 1) * BLK)
        back = aggregate(layers % 2, b).astype(BF16)
        grad_initial[0, rows, :] = grad_initial[0, rows, :] + back.astype(F32)


def run_layers(scale, betas, pieces, weights):
    vmem = pl.BlockSpec(memory_space=pltpu.VMEM)
    nodes, width = 2048, 256
    return pl.pallas_call(
        functools.partial(layers_kernel, scale, betas),
        in_specs=[vmem] * (len(pieces) + len(weights)),
        out_specs=[vmem, vmem],
        out_shape=[
            jax.ShapeDtypeStruct((1, 256, width), F32),
            jax.ShapeDtypeStruct((4, 64, width), BF16),
        ],
        scratch_shapes=[
            pltpu.VMEM((nodes, width), F32),
            pltpu.VMEM((4, width, width), BF16),
            pltpu.VMEM((8, BLK), jnp.int32),
            pltpu.SMEM((8, BLK), jnp.int32),
            pltpu.VMEM((nodes, width), BF16),
            pltpu.VMEM((nodes, width), BF16),
            pltpu.VMEM((4, nodes, width), BF16),
            pltpu.VMEM((4, nodes, width), F32),
            pltpu.VMEM((nodes, width), BF16),
            pltpu.VMEM((BLK, width), F32),
            pltpu.SemaphoreType.DMA,
        ],
        compiler_params=pltpu.CompilerParams(vmem_limit_bytes=40 * 1024 * 1024),
        cost_estimate=pl.CostEstimate(flops=9_000_000_000, bytes_accessed=6_000_000, transcendentals=0),
        name="layers",
    )(*pieces, *weights)


def onward(v):
    route = [(i, (i + 2) % 8 if i % 2 == 0 else (i - 2) % 8) for i in range(8)]
    return lax.ppermute(v, "dom", route)


def other_core(v):
    return lax.ppermute(v, "dom", [(i, i ^ 1) for i in range(8)])


def phase_weights(w):
    return [w] + [lax.ppermute(w, "phase", [(i, (i + n) % 4) for i in range(4)]) for n in (1, 2, 3)]


def across(v):
    route = [(i, (i + 2) % 8 - 1 if i % 2 else (i - 2) % 8 + 1) for i in range(8)]
    return lax.ppermute(v, "dom", route)


def gather(own, w):
    near, near_too = onward(own), across(own)
    partner = other_core(own)
    weights = phase_weights(w)
    early, *weights = lax.optimization_barrier((near, *weights))
    far = onward(early)
    pieces = [own, partner, near, near_too, far, other_core(far), other_core(near_too), other_core(near)]
    return pieces, weights


def local(initial, block_cols, block_tiles, layer_weights, cotangent):
    layers = lax.axis_size("phase")
    nodes_all = 4 * 2048 * lax.axis_size("dp")
    scale = 1.0 / math.sqrt(nodes_all)
    betas = [math.log(THETA / (l + 1) + 1.0) for l in range(layers)]
    spans, rows = block_tiles.shape[:2]
    tiles = block_tiles.reshape(spans, rows * NZB * BLK, BLK)
    own = pack(tiles, initial, cotangent, block_cols)
    pieces, weights = gather(own, layer_weights)
    grad_initial, parts = run_layers(scale, betas, pieces, weights)
    parts = lax.all_to_all(parts, "phase", 0, 0, tiled=True)
    mine = jnp.sum(parts.astype(F32), axis=0).astype(BF16)
    mine = jnp.broadcast_to(mine[None], (8,) + mine.shape)
    mine = jnp.sum(lax.all_to_all(mine, "dp", 0, 0, tiled=True).astype(F32), axis=0)
    dom = lax.axis_index("dom")
    for bit in (2, 1):
        other = lax.ppermute(mine, "dom", [(i, i ^ bit) for i in range(8)])
        odd = lax.bitwise_and(dom, bit) != 0
        both = jnp.stack([jnp.where(odd, other, mine), jnp.where(odd, mine, other)])
        mine = both.reshape(-1, both.shape[-1])
    return grad_initial, mine.reshape(1, 256, 256)


def solution(mesh):
    placed = (
        P("dp", "dom", None),
        P("dp", "dom", None),
        P("dp", "dom", None, None, None),
        P("phase", None, None),
        P("dp", "dom", None),
    )
    return jax.shard_map(
        local,
        mesh=mesh,
        in_specs=placed,
        out_specs=(P(("dp", "phase"), "dom", None), P("phase", None, None)),
        check_vma=False,
    )
```

```python
import functools
import math

import jax
import jax.numpy as jnp
from jax import lax
from jax.experimental import pallas as pl
from jax.experimental.pallas import tpu as pltpu
from jax.sharding import PartitionSpec as P

ALPHA = 0.1
THETA = 0.5
BLK = 128
NZB = 5
GELU_C = math.sqrt(2.0 / math.pi)
GELU_B = 0.044715
ROWS = 2 * BLK
TILE_ROWS = 2 * NZB * BLK
START = TILE_ROWS
COT = START + 2 * ROWS
COLS = COT + 2 * ROWS
PIECE = COLS + 16
CHUNK = 4
LAG = 8
GELU_C = math.sqrt(2.0 / math.pi)
GELU_B = 0.044715
HEAD_TILES = 7
TAIL_START = (2 * NZB - HEAD_TILES) * BLK
TAIL_COLS = TAIL_START + 512
CHUNK = 4
LAG = 8
BF16 = jnp.bfloat16
F32 = jnp.float32


def pack_kernel(tiles, initial, cotangent, cols, piece, start, cot, sems):
    span = lax.axis_index("phase")
    copies = [
        (initial.at[span], start),
        (cotangent.at[span], cot),
        (tiles.at[span], piece.at[pl.ds(0, TILE_ROWS)]),
    ]
    started = [pltpu.make_async_copy(a, b, sems.at[n]) for n, (a, b) in enumerate(copies)]
    for c in started:
        c.start()
    lane = lax.broadcasted_iota(jnp.int32, (16, BLK), 1)
    vec = jnp.zeros((16, BLK), F32)
    for b in range(2):
        for k in range(NZB):
            vec = jnp.where(lane == b * NZB + k, cols[span, b, k].astype(F32), vec)
    piece[COLS : COLS + 16, :] = vec.astype(BF16)
    for copy, base, array in ((started[0], START, start), (started[1], COT, cot)):
        copy.wait()
        piece[base : base + ROWS, :] = array[:, :BLK]
        piece[base + ROWS : base + 2 * ROWS, :] = array[:, BLK:]
    started[2].wait()


def pack(tiles, initial, cotangent, cols):
    any_spec = pl.BlockSpec(memory_space=pl.ANY)
    return pl.pallas_call(
        pack_kernel,
        in_specs=[any_spec, any_spec, any_spec, pl.BlockSpec(memory_space=pltpu.SMEM)],
        out_specs=pl.BlockSpec(memory_space=pltpu.VMEM),
        out_shape=pltpu.VMEM((PIECE, BLK), BF16),
        scratch_shapes=[
            pltpu.VMEM((ROWS, 2 * BLK), BF16),
            pltpu.VMEM((ROWS, 2 * BLK), BF16),
            pltpu.SemaphoreType.DMA((3,)),
        ],
        name="pack",
    )(*[pltpu.with_memory_space_constraint(a, pltpu.HBM) for a in (tiles, initial, cotangent)], cols)


def dot(a, b, dims):
    return lax.dot_general(a, b, (dims, ((), ())), preferred_element_type=F32)


def layers_kernel(scale, betas, *refs):
    layers = len(betas)
    pieces, weights = refs[:8], refs[8 : 8 + layers]
    grad_initial, grad_weights = refs[8 + layers : 10 + layers]
    start, weight, cols_int, cols, h_even, h_odd, mixes, slopes, dpre, dw, sem = refs[10 + layers :]

    hidden = (h_even, h_odd)

    def piece(n, low, rows):
        return pieces[n][low : low + rows, :]

    dom = lax.axis_index("dom")
    phase = lax.axis_index("phase")
    x, core = dom // 2, dom % 2
    for n in range(layers):
        weight[(phase - n + layers) % layers] = weights[n][0]
    way = 1 - 2 * core
    for n in range(8):
        j = piece(n, COLS, 16).astype(F32).astype(jnp.int32)
        chip = lax.bitwise_and(way * (x - lax.shift_right_logical(j, 2)) + 4, 3)
        side = lax.bitwise_xor(lax.bitwise_and(lax.shift_right_logical(j, 1), 1), core)
        place = chip * 4 + side * 2 + lax.bitwise_and(j, 1)
        cols_int[n : n + 1, :] = (place * BLK)[:1]
    to_scalars = pltpu.make_async_copy(cols_int, cols, sem)
    to_scalars.start()
    for n in range(8):
        for half in range(2):
            part = piece(n, START + ROWS * half, ROWS)
            lanes = slice(BLK * half, BLK * (half + 1))
            h_even[ROWS * n : ROWS * (n + 1), lanes] = part
            start[ROWS * n : ROWS * (n + 1), lanes] = ALPHA * part.astype(F32)
    to_scalars.wait()

    def tile(i, k):
        return piece(i // 2, ((i % 2) * NZB + k) * BLK, BLK)

    def aggregate(src, i):
        blocks = [hidden[src][i * BLK : (i + 1) * BLK, :]]
        for k in range(1, NZB):
            j = pl.multiple_of(cols[i // 2, (i % 2) * NZB + k], BLK)
            blocks.append(hidden[src][pl.ds(j, BLK), :])
        lhs = jnp.concatenate([tile(i, k) for k in range(NZB)], axis=1)
        return (1.0 - ALPHA) * dot(lhs, jnp.concatenate(blocks, axis=0), ((1,), (0,)))

    blocks_all = start.shape[0] // BLK

    def pipeline(first, second, third):
        held = {}
        for s in range(blocks_all + LAG):
            if s < blocks_all:
                first(s)
            if s < blocks_all + CHUNK and s >= CHUNK and s % CHUNK == 0:
                held[s // CHUNK - 1] = second(s // CHUNK - 1)
            i = s - LAG
            if 0 <= i < blocks_all:
                product = held[i // CHUNK]
                third(i, product[(i % CHUNK) * BLK : (i % CHUNK + 1) * BLK, :])

    def pick(values, l):
        if isinstance(l, int):
            return values[l]
        out = jnp.float32(values[0])
        for n in range(1, len(values)):
            out = jnp.where(l == n, jnp.float32(values[n]), out)
        return out

    def forward(l, src):
        dst = 1 - src
        beta = pick(betas, l)
        w = weight[l]

        def first(i):
            rows = slice(i * BLK, (i + 1) * BLK)
            mixes[l, rows, :] = (aggregate(src, i) + start[rows, :]).astype(BF16)

        def second(c):
            return dot(mixes[l, c * CHUNK * BLK : (c + 1) * CHUNK * BLK, :], w, ((1,), (0,)))

        def third(i, product):
            rows = slice(i * BLK, (i + 1) * BLK)
            pre = (1.0 - beta) * mixes[l, rows, :].astype(F32) + beta * product
            square = pre * pre
            t = jnp.tanh(pre * (GELU_C + (GELU_C * GELU_B) * square))
            half = 0.5 + 0.5 * t
            out = pre * half
            hidden[dst][rows, :] = out.astype(BF16)
            slopes[l, rows, :] = half + out * (1.0 - half) * (
                2.0 * GELU_C + (6.0 * GELU_C * GELU_B) * square
            )

        pipeline(first, second, third)
        return 0

    def backward(step, src, top=False):
        l = layers - 1 - step
        dst = 1 - src
        beta = pick(betas, l)
        w = weight[l]

        def first(i):
            rows = slice(i * BLK, (i + 1) * BLK)
            if top:
                low = COT + (i % 2) * BLK
                back = jnp.concatenate([piece(i // 2, low, BLK), piece(i // 2, low + ROWS, BLK)], axis=1)
            else:
                back = aggregate(src, i).astype(BF16)
            dpre[rows, :] = (slopes[l, rows, :] * back.astype(F32)).astype(BF16)

        def second(c):
            return dot(dpre[c * CHUNK * BLK : (c + 1) * CHUNK * BLK, :], w, ((1,), (1,)))

        def third(i, product):
            rows = slice(i * BLK, (i + 1) * BLK)
            dmix = (1.0 - beta) * dpre[rows, :].astype(F32) + beta * product
            hidden[dst][rows, :] = dmix.astype(BF16)

        pipeline(first, second, third)
        term = ALPHA * hidden[dst][0:256, :].astype(F32)
        grad_initial[0] = term if top else grad_initial[0] + term
        lanes = pl.ds(pl.multiple_of(core * BLK, BLK), BLK)
        dw[...] = (beta * scale) * dot(mixes[l, :, lanes], dpre[...], ((0,), (0,)))
        grad_weights[(l - phase + layers) % layers] = dw[pl.ds(pl.multiple_of(x % 2 * 64, 64), 64), :].astype(BF16)
        return 0

    def two_forward(m, _):
        forward(2 * m, 0)
        forward(2 * m + 1, 1)
        return 0

    def two_backward(m, _):
        backward(2 * m, 0)
        backward(2 * m + 1, 1)
        return 0

    lax.fori_loop(0, layers // 2, two_forward, 0)
    backward(0, 0, top=True)
    backward(1, 1)
    lax.fori_loop(1, layers // 2, two_backward, 0)
    for b in range(2):
        rows = slice(b * BLK, (b + 1) * BLK)
        back = aggregate(layers % 2, b).astype(BF16)
        grad_initial[0, rows, :] = grad_initial[0, rows, :] + back.astype(F32)


def run_layers(scale, betas, pieces, weights):
    vmem = pl.BlockSpec(memory_space=pltpu.VMEM)
    nodes, width = 2048, 256
    return pl.pallas_call(
        functools.partial(layers_kernel, scale, betas),
        in_specs=[vmem] * (len(pieces) + len(weights)),
        out_specs=[vmem, vmem],
        out_shape=[
            jax.ShapeDtypeStruct((1, 256, width), F32),
            jax.ShapeDtypeStruct((4, 64, width), BF16),
        ],
        scratch_shapes=[
            pltpu.VMEM((nodes, width), F32),
            pltpu.VMEM((4, width, width), BF16),
            pltpu.VMEM((8, BLK), jnp.int32),
            pltpu.SMEM((8, BLK), jnp.int32),
            pltpu.VMEM((nodes, width), BF16),
            pltpu.VMEM((nodes, width), BF16),
            pltpu.VMEM((4, nodes, width), BF16),
            pltpu.VMEM((4, nodes, width), F32),
            pltpu.VMEM((nodes, width), BF16),
            pltpu.VMEM((BLK, width), F32),
            pltpu.SemaphoreType.DMA,
        ],
        compiler_params=pltpu.CompilerParams(vmem_limit_bytes=40 * 1024 * 1024),
        cost_estimate=pl.CostEstimate(flops=9_000_000_000, bytes_accessed=6_000_000, transcendentals=0),
        name="layers",
    )(*pieces, *weights)


def onward(v):
    route = [(i, (i + 2) % 8 if i % 2 == 0 else (i - 2) % 8) for i in range(8)]
    return lax.ppermute(v, "dom", route)


def other_core(v):
    return lax.ppermute(v, "dom", [(i, i ^ 1) for i in range(8)])


def to_phase(v, n):
    return lax.ppermute(v, "phase", [(i, (i + n) % 4) for i in range(4)])


def across(v):
    route = [(i, (i + 2) % 8 - 1 if i % 2 else (i - 2) % 8 + 1) for i in range(8)]
    return lax.ppermute(v, "dom", route)


def gather(own, w):
    near, near_too = onward(own), across(own)
    partner = other_core(own)
    weights = [w] + [to_phase(w, n) for n in (1, 2, 3)]
    early, *weights = lax.optimization_barrier((near, *weights))
    far = onward(early)
    pieces = [own, partner, near, near_too, far, other_core(far), other_core(near_too), other_core(near)]
    return pieces, weights


def local(initial, block_cols, block_tiles, layer_weights, cotangent):
    layers = lax.axis_size("phase")
    nodes_all = 4 * 2048 * lax.axis_size("dp")
    scale = 1.0 / math.sqrt(nodes_all)
    betas = [math.log(THETA / (l + 1) + 1.0) for l in range(layers)]
    spans, rows = block_tiles.shape[:2]
    tiles = block_tiles.reshape(spans, rows * NZB * BLK, BLK)
    own = pack(tiles, initial, cotangent, block_cols)
    pieces, weights = gather(own, layer_weights)
    grad_initial, parts = run_layers(scale, betas, pieces, weights)
    mine = parts[0].astype(F32)
    for n in (1, 2, 3):
        mine = mine + to_phase(parts[n], n).astype(F32)
    mine = mine.astype(BF16)
    mine = jnp.broadcast_to(mine[None], (8,) + mine.shape)
    mine = jnp.sum(lax.all_to_all(mine, "dp", 0, 0, tiled=True).astype(F32), axis=0)
    dom = lax.axis_index("dom")
    for bit in (2, 1):
        other = lax.ppermute(mine, "dom", [(i, i ^ bit) for i in range(8)])
        odd = lax.bitwise_and(dom, bit) != 0
        both = jnp.stack([jnp.where(odd, other, mine), jnp.where(odd, mine, other)])
        mine = both.reshape(-1, both.shape[-1])
    return grad_initial, mine.reshape(1, 256, 256)


def solution(mesh):
    placed = (
        P("dp", "dom", None),
        P("dp", "dom", None),
        P("dp", "dom", None, None, None),
        P("phase", None, None),
        P("dp", "dom", None),
    )
    return jax.shard_map(
        local,
        mesh=mesh,
        in_specs=placed,
        out_specs=(P(("dp", "phase"), "dom", None), P("phase", None, None)),
        check_vma=False,
    )
```

```python
import functools
import math

import jax
import jax.numpy as jnp
from jax import lax
from jax.experimental import pallas as pl
from jax.experimental.pallas import tpu as pltpu
from jax.sharding import PartitionSpec as P

ALPHA = 0.1
THETA = 0.5
BLK = 128
NZB = 5
GELU_C = math.sqrt(2.0 / math.pi)
GELU_B = 0.044715
ROWS = 2 * BLK
TILE_ROWS = 2 * NZB * BLK
START = TILE_ROWS
COT = START + 2 * ROWS
COLS = COT + 2 * ROWS
PIECE = COLS + 16
CHUNK = 4
LAG = 8
GELU_C = math.sqrt(2.0 / math.pi)
GELU_B = 0.044715
HEAD_TILES = 7
TAIL_START = (2 * NZB - HEAD_TILES) * BLK
TAIL_COLS = TAIL_START + 512
CHUNK = 4
LAG = 8
BF16 = jnp.bfloat16
F32 = jnp.float32


def pack_kernel(tiles, initial, cotangent, cols, piece, start, cot, sems):
    span = lax.axis_index("phase")
    copies = [
        (initial.at[span], start),
        (cotangent.at[span], cot),
        (tiles.at[span], piece.at[pl.ds(0, TILE_ROWS)]),
    ]
    started = [pltpu.make_async_copy(a, b, sems.at[n]) for n, (a, b) in enumerate(copies)]
    for c in started:
        c.start()
    lane = lax.broadcasted_iota(jnp.int32, (16, BLK), 1)
    vec = jnp.zeros((16, BLK), F32)
    for b in range(2):
        for k in range(NZB):
            vec = jnp.where(lane == b * NZB + k, cols[span, b, k].astype(F32), vec)
    piece[COLS : COLS + 16, :] = vec.astype(BF16)
    for copy, base, array in ((started[0], START, start), (started[1], COT, cot)):
        copy.wait()
        piece[base : base + ROWS, :] = array[:, :BLK]
        piece[base + ROWS : base + 2 * ROWS, :] = array[:, BLK:]
    started[2].wait()


def pack(tiles, initial, cotangent, cols):
    any_spec = pl.BlockSpec(memory_space=pl.ANY)
    return pl.pallas_call(
        pack_kernel,
        in_specs=[any_spec, any_spec, any_spec, pl.BlockSpec(memory_space=pltpu.SMEM)],
        out_specs=pl.BlockSpec(memory_space=pltpu.VMEM),
        out_shape=pltpu.VMEM((PIECE, BLK), BF16),
        scratch_shapes=[
            pltpu.VMEM((ROWS, 2 * BLK), BF16),
            pltpu.VMEM((ROWS, 2 * BLK), BF16),
            pltpu.SemaphoreType.DMA((3,)),
        ],
        name="pack",
    )(*[pltpu.with_memory_space_constraint(a, pltpu.HBM) for a in (tiles, initial, cotangent)], cols)


def dot(a, b, dims):
    return lax.dot_general(a, b, (dims, ((), ())), preferred_element_type=F32)


def layers_kernel(scale, betas, *refs):
    layers = len(betas)
    pieces, weights = refs[:8], refs[8 : 8 + layers]
    grad_initial, grad_weights = refs[8 + layers : 10 + layers]
    start, weight, cols_int, cols, h_even, h_odd, mixes, slopes, dpre, dw, sem = refs[10 + layers :]

    hidden = (h_even, h_odd)

    def piece(n, low, rows):
        return pieces[n][low : low + rows, :]

    dom = lax.axis_index("dom")
    phase = lax.axis_index("phase")
    x, core = dom // 2, dom % 2
    for n in range(layers):
        weight[(phase - n + layers) % layers] = weights[n][0]
    way = 1 - 2 * core
    for n in range(8):
        j = piece(n, COLS, 16).astype(F32).astype(jnp.int32)
        chip = lax.bitwise_and(way * (x - lax.shift_right_logical(j, 2)) + 4, 3)
        side = lax.bitwise_xor(lax.bitwise_and(lax.shift_right_logical(j, 1), 1), core)
        place = chip * 4 + side * 2 + lax.bitwise_and(j, 1)
        cols_int[n : n + 1, :] = (place * BLK)[:1]
    to_scalars = pltpu.make_async_copy(cols_int, cols, sem)
    to_scalars.start()
    for n in range(8):
        for half in range(2):
            part = piece(n, START + ROWS * half, ROWS)
            lanes = slice(BLK * half, BLK * (half + 1))
            h_even[ROWS * n : ROWS * (n + 1), lanes] = part
            start[ROWS * n : ROWS * (n + 1), lanes] = ALPHA * part.astype(F32)
    to_scalars.wait()

    def tile(i, k):
        return piece(i // 2, ((i % 2) * NZB + k) * BLK, BLK)

    def aggregate(src, i):
        blocks = [hidden[src][i * BLK : (i + 1) * BLK, :]]
        for k in range(1, NZB):
            j = pl.multiple_of(cols[i // 2, (i % 2) * NZB + k], BLK)
            blocks.append(hidden[src][pl.ds(j, BLK), :])
        lhs = jnp.concatenate([tile(i, k) for k in range(NZB)], axis=1)
        return (1.0 - ALPHA) * dot(lhs, jnp.concatenate(blocks, axis=0), ((1,), (0,)))

    blocks_all = start.shape[0] // BLK

    def pipeline(first, second, third):
        held = {}
        for s in range(blocks_all + LAG):
            if s < blocks_all:
                first(s)
            if s < blocks_all + CHUNK and s >= CHUNK and s % CHUNK == 0:
                held[s // CHUNK - 1] = second(s // CHUNK - 1)
            i = s - LAG
            if 0 <= i < blocks_all:
                product = held[i // CHUNK]
                third(i, product[(i % CHUNK) * BLK : (i % CHUNK + 1) * BLK, :])

    def pick(values, l):
        if isinstance(l, int):
            return values[l]
        out = jnp.float32(values[0])
        for n in range(1, len(values)):
            out = jnp.where(l == n, jnp.float32(values[n]), out)
        return out

    def forward(l, src):
        dst = 1 - src
        beta = pick(betas, l)
        w = weight[l]

        def first(i):
            rows = slice(i * BLK, (i + 1) * BLK)
            mixes[l, rows, :] = (aggregate(src, i) + start[rows, :]).astype(BF16)

        def second(c):
            return dot(mixes[l, c * CHUNK * BLK : (c + 1) * CHUNK * BLK, :], w, ((1,), (0,)))

        def third(i, product):
            rows = slice(i * BLK, (i + 1) * BLK)
            pre = (1.0 - beta) * mixes[l, rows, :].astype(F32) + beta * product
            square = pre * pre
            t = jnp.tanh(pre * (GELU_C + (GELU_C * GELU_B) * square))
            half = 0.5 + 0.5 * t
            out = pre * half
            hidden[dst][rows, :] = out.astype(BF16)
            slopes[l, rows, :] = half + out * (1.0 - half) * (
                2.0 * GELU_C + (6.0 * GELU_C * GELU_B) * square
            )

        pipeline(first, second, third)
        return 0

    def backward(step, src, top=False):
        l = layers - 1 - step
        dst = 1 - src
        beta = pick(betas, l)
        w = weight[l]

        def first(i):
            rows = slice(i * BLK, (i + 1) * BLK)
            if top:
                low = COT + (i % 2) * BLK
                back = jnp.concatenate([piece(i // 2, low, BLK), piece(i // 2, low + ROWS, BLK)], axis=1)
            else:
                back = aggregate(src, i).astype(BF16)
            dpre[rows, :] = (slopes[l, rows, :] * back.astype(F32)).astype(BF16)

        def second(c):
            return dot(dpre[c * CHUNK * BLK : (c + 1) * CHUNK * BLK, :], w, ((1,), (1,)))

        def third(i, product):
            rows = slice(i * BLK, (i + 1) * BLK)
            dmix = (1.0 - beta) * dpre[rows, :].astype(F32) + beta * product
            hidden[dst][rows, :] = dmix.astype(BF16)

        pipeline(first, second, third)
        term = ALPHA * hidden[dst][0:256, :].astype(F32)
        grad_initial[0] = term if top else grad_initial[0] + term
        lanes = pl.ds(pl.multiple_of(core * BLK, BLK), BLK)
        dw[...] = (beta * scale) * dot(mixes[l, :, lanes], dpre[...], ((0,), (0,)))
        grad_weights[(l - phase + layers) % layers] = dw[pl.ds(pl.multiple_of(x % 2 * 64, 64), 64), :].astype(BF16)
        return 0

    def two_forward(m, _):
        forward(2 * m, 0)
        forward(2 * m + 1, 1)
        return 0

    def two_backward(m, _):
        backward(2 * m, 0)
        backward(2 * m + 1, 1)
        return 0

    lax.fori_loop(0, layers // 2, two_forward, 0)
    backward(0, 0, top=True)
    backward(1, 1)
    lax.fori_loop(1, layers // 2, two_backward, 0)
    for b in range(2):
        rows = slice(b * BLK, (b + 1) * BLK)
        back = aggregate(layers % 2, b).astype(BF16)
        grad_initial[0, rows, :] = grad_initial[0, rows, :] + back.astype(F32)


def run_layers(scale, betas, pieces, weights):
    vmem = pl.BlockSpec(memory_space=pltpu.VMEM)
    nodes, width = 2048, 256
    return pl.pallas_call(
        functools.partial(layers_kernel, scale, betas),
        in_specs=[vmem] * (len(pieces) + len(weights)),
        out_specs=[vmem, vmem],
        out_shape=[
            jax.ShapeDtypeStruct((1, 256, width), F32),
            jax.ShapeDtypeStruct((4, 64, width), BF16),
        ],
        scratch_shapes=[
            pltpu.VMEM((nodes, width), F32),
            pltpu.VMEM((4, width, width), BF16),
            pltpu.VMEM((8, BLK), jnp.int32),
            pltpu.SMEM((8, BLK), jnp.int32),
            pltpu.VMEM((nodes, width), BF16),
            pltpu.VMEM((nodes, width), BF16),
            pltpu.VMEM((4, nodes, width), BF16),
            pltpu.VMEM((4, nodes, width), F32),
            pltpu.VMEM((nodes, width), BF16),
            pltpu.VMEM((BLK, width), F32),
            pltpu.SemaphoreType.DMA,
        ],
        compiler_params=pltpu.CompilerParams(vmem_limit_bytes=40 * 1024 * 1024),
        cost_estimate=pl.CostEstimate(flops=9_000_000_000, bytes_accessed=6_000_000, transcendentals=0),
        name="layers",
    )(*pieces, *weights)


def onward(v):
    route = [(i, (i + 2) % 8 if i % 2 == 0 else (i - 2) % 8) for i in range(8)]
    return lax.ppermute(v, "dom", route)


def other_core(v):
    return lax.ppermute(v, "dom", [(i, i ^ 1) for i in range(8)])


def to_phase(v, n):
    return lax.ppermute(v, "phase", [(i, (i + n) % 4) for i in range(4)])


def across(v):
    route = [(i, (i + 2) % 8 - 1 if i % 2 else (i - 2) % 8 + 1) for i in range(8)]
    return lax.ppermute(v, "dom", route)


def gather(own, w):
    near, near_too = onward(own), across(own)
    partner = other_core(own)
    weights = [w] + [to_phase(w, n) for n in (1, 2, 3)]
    early, *weights = lax.optimization_barrier((near, *weights))
    far = onward(early)
    pieces = [own, partner, near, near_too, far, other_core(far), other_core(near_too), other_core(near)]
    return pieces, weights


def local(initial, block_cols, block_tiles, layer_weights, cotangent):
    layers = lax.axis_size("phase")
    nodes_all = 4 * 2048 * lax.axis_size("dp")
    scale = 1.0 / math.sqrt(nodes_all)
    betas = [math.log(THETA / (l + 1) + 1.0) for l in range(layers)]
    spans, rows = block_tiles.shape[:2]
    tiles = block_tiles.reshape(spans, rows * NZB * BLK, BLK)
    own = pack(tiles, initial, cotangent, block_cols)
    pieces, weights = gather(own, layer_weights)
    grad_initial, parts = run_layers(scale, betas, pieces, weights)
    mine = parts[0].astype(F32)
    for n in (1, 2, 3):
        mine = mine + to_phase(parts[n], n).astype(F32)
    mine = mine.astype(BF16)
    mine = jnp.broadcast_to(mine[None], (8,) + mine.shape)
    mine = jnp.sum(lax.all_to_all(mine, "dp", 0, 0, tiled=True).astype(F32), axis=0)
    dom = lax.axis_index("dom")
    held = [mine] + [lax.ppermute(mine, "dom", [(i, i ^ n) for i in range(8)]) for n in (2, 3, 1)]
    by_bits = {0: held[0], 2: held[1], 3: held[2], 1: held[3]}
    far_chip, far_core = lax.bitwise_and(dom, 2) != 0, lax.bitwise_and(dom, 1) != 0
    rows = []
    for quarter in (0, 2, 1, 3):
        chip = [jnp.where(far_chip, by_bits[quarter ^ 2 ^ n], by_bits[quarter ^ n]) for n in (0, 1)]
        rows.append(jnp.where(far_core, chip[1], chip[0]))
    return grad_initial, jnp.concatenate(rows, axis=0)[None]


def solution(mesh):
    placed = (
        P("dp", "dom", None),
        P("dp", "dom", None),
        P("dp", "dom", None, None, None),
        P("phase", None, None),
        P("dp", "dom", None),
    )
    return jax.shard_map(
        local,
        mesh=mesh,
        in_specs=placed,
        out_specs=(P(("dp", "phase"), "dom", None), P("phase", None, None)),
        check_vma=False,
    )
```

```python
import functools
import math

import jax
import jax.numpy as jnp
from jax import lax
from jax.experimental import pallas as pl
from jax.experimental.pallas import tpu as pltpu
from jax.sharding import PartitionSpec as P

ALPHA = 0.1
THETA = 0.5
BLK = 128
NZB = 5
GELU_C = math.sqrt(2.0 / math.pi)
GELU_B = 0.044715
ROWS = 2 * BLK
TILE_ROWS = 2 * NZB * BLK
START = TILE_ROWS
COT = START + 2 * ROWS
COLS = COT + 2 * ROWS
PIECE = COLS + 16
CHUNK = 4
LAG = 8
GELU_C = math.sqrt(2.0 / math.pi)
GELU_B = 0.044715
HEAD_TILES = 7
TAIL_START = (2 * NZB - HEAD_TILES) * BLK
TAIL_COLS = TAIL_START + 512
CHUNK = 4
LAG = 8
BF16 = jnp.bfloat16
F32 = jnp.float32


def pack_kernel(tiles, initial, cotangent, cols, piece, start, cot, sems):
    span = lax.axis_index("phase")
    copies = [
        (initial.at[span], start),
        (cotangent.at[span], cot),
        (tiles.at[span], piece.at[pl.ds(0, TILE_ROWS)]),
    ]
    started = [pltpu.make_async_copy(a, b, sems.at[n]) for n, (a, b) in enumerate(copies)]
    for c in started:
        c.start()
    lane = lax.broadcasted_iota(jnp.int32, (16, BLK), 1)
    vec = jnp.zeros((16, BLK), F32)
    for b in range(2):
        for k in range(NZB):
            vec = jnp.where(lane == b * NZB + k, cols[span, b, k].astype(F32), vec)
    piece[COLS : COLS + 16, :] = vec.astype(BF16)
    for copy, base, array in ((started[0], START, start), (started[1], COT, cot)):
        copy.wait()
        piece[base : base + ROWS, :] = array[:, :BLK]
        piece[base + ROWS : base + 2 * ROWS, :] = array[:, BLK:]
    started[2].wait()


def pack(tiles, initial, cotangent, cols):
    any_spec = pl.BlockSpec(memory_space=pl.ANY)
    return pl.pallas_call(
        pack_kernel,
        in_specs=[any_spec, any_spec, any_spec, pl.BlockSpec(memory_space=pltpu.SMEM)],
        out_specs=pl.BlockSpec(memory_space=pltpu.VMEM),
        out_shape=pltpu.VMEM((PIECE, BLK), BF16),
        scratch_shapes=[
            pltpu.VMEM((ROWS, 2 * BLK), BF16),
            pltpu.VMEM((ROWS, 2 * BLK), BF16),
            pltpu.SemaphoreType.DMA((3,)),
        ],
        name="pack",
    )(*[pltpu.with_memory_space_constraint(a, pltpu.HBM) for a in (tiles, initial, cotangent)], cols)


def dot(a, b, dims):
    return lax.dot_general(a, b, (dims, ((), ())), preferred_element_type=F32)


def layers_kernel(scale, betas, *refs):
    layers = len(betas)
    pieces, weights = refs[:8], refs[8 : 8 + layers]
    grad_initial, grad_weights = refs[8 + layers : 10 + layers]
    start, weight, cols_int, cols, h_even, h_odd, mixes, slopes, dpre, dw, sem = refs[10 + layers :]

    hidden = (h_even, h_odd)

    def piece(n, low, rows):
        return pieces[n][low : low + rows, :]

    dom = lax.axis_index("dom")
    phase = lax.axis_index("phase")
    x, core = dom // 2, dom % 2
    for n in range(layers):
        weight[(phase - n + layers) % layers] = weights[n][0]
    way = 1 - 2 * core
    for n in range(8):
        j = piece(n, COLS, 16).astype(F32).astype(jnp.int32)
        chip = lax.bitwise_and(way * (x - lax.shift_right_logical(j, 2)) + 4, 3)
        side = lax.bitwise_xor(lax.bitwise_and(lax.shift_right_logical(j, 1), 1), core)
        place = chip * 4 + side * 2 + lax.bitwise_and(j, 1)
        cols_int[n : n + 1, :] = (place * BLK)[:1]
    to_scalars = pltpu.make_async_copy(cols_int, cols, sem)
    to_scalars.start()
    for n in range(8):
        for half in range(2):
            part = piece(n, START + ROWS * half, ROWS)
            lanes = slice(BLK * half, BLK * (half + 1))
            h_even[ROWS * n : ROWS * (n + 1), lanes] = part
            start[ROWS * n : ROWS * (n + 1), lanes] = ALPHA * part.astype(F32)
    to_scalars.wait()

    def tile(i, k):
        return piece(i // 2, ((i % 2) * NZB + k) * BLK, BLK)

    def aggregate(src, i):
        blocks = [hidden[src][i * BLK : (i + 1) * BLK, :]]
        for k in range(1, NZB):
            j = pl.multiple_of(cols[i // 2, (i % 2) * NZB + k], BLK)
            blocks.append(hidden[src][pl.ds(j, BLK), :])
        lhs = jnp.concatenate([tile(i, k) for k in range(NZB)], axis=1)
        return (1.0 - ALPHA) * dot(lhs, jnp.concatenate(blocks, axis=0), ((1,), (0,)))

    blocks_all = start.shape[0] // BLK

    def pipeline(first, second, third):
        held = {}
        for s in range(blocks_all + LAG):
            if s < blocks_all:
                first(s)
            if s < blocks_all + CHUNK and s >= CHUNK and s % CHUNK == 0:
                held[s // CHUNK - 1] = second(s // CHUNK - 1)
            i = s - LAG
            if 0 <= i < blocks_all:
                product = held[i // CHUNK]
                third(i, product[(i % CHUNK) * BLK : (i % CHUNK + 1) * BLK, :])

    def pick(values, l):
        if isinstance(l, int):
            return values[l]
        out = jnp.float32(values[0])
        for n in range(1, len(values)):
            out = jnp.where(l == n, jnp.float32(values[n]), out)
        return out

    def forward(l, src):
        dst = 1 - src
        beta = pick(betas, l)
        w = weight[l]

        def first(i):
            rows = slice(i * BLK, (i + 1) * BLK)
            mixes[l, rows, :] = (aggregate(src, i) + start[rows, :]).astype(BF16)

        def second(c):
            return dot(mixes[l, c * CHUNK * BLK : (c + 1) * CHUNK * BLK, :], w, ((1,), (0,)))

        def third(i, product):
            rows = slice(i * BLK, (i + 1) * BLK)
            pre = (1.0 - beta) * mixes[l, rows, :].astype(F32) + beta * product
            square = pre * pre
            t = jnp.tanh(pre * (GELU_C + (GELU_C * GELU_B) * square))
            half = 0.5 + 0.5 * t
            out = pre * half
            hidden[dst][rows, :] = out.astype(BF16)
            slopes[l, rows, :] = half + out * (1.0 - half) * (
                2.0 * GELU_C + (6.0 * GELU_C * GELU_B) * square
            )

        pipeline(first, second, third)
        return 0

    def backward(step, src, top=False):
        l = layers - 1 - step
        dst = 1 - src
        beta = pick(betas, l)
        w = weight[l]

        def first(i):
            rows = slice(i * BLK, (i + 1) * BLK)
            if top:
                low = COT + (i % 2) * BLK
                back = jnp.concatenate([piece(i // 2, low, BLK), piece(i // 2, low + ROWS, BLK)], axis=1)
            else:
                back = aggregate(src, i).astype(BF16)
            dpre[rows, :] = (slopes[l, rows, :] * back.astype(F32)).astype(BF16)

        def second(c):
            return dot(dpre[c * CHUNK * BLK : (c + 1) * CHUNK * BLK, :], w, ((1,), (1,)))

        def third(i, product):
            rows = slice(i * BLK, (i + 1) * BLK)
            dmix = (1.0 - beta) * dpre[rows, :].astype(F32) + beta * product
            hidden[dst][rows, :] = dmix.astype(BF16)

        pipeline(first, second, third)
        term = ALPHA * hidden[dst][0:256, :].astype(F32)
        grad_initial[0] = term if top else grad_initial[0] + term
        lanes = pl.ds(pl.multiple_of(core * BLK, BLK), BLK)
        dw[...] = (beta * scale) * dot(mixes[l, :, lanes], dpre[...], ((0,), (0,)))
        grad_weights[(l - phase + layers) % layers] = dw[pl.ds(pl.multiple_of(x % 2 * 64, 64), 64), :].astype(BF16)
        return 0

    def two_forward(m, _):
        forward(2 * m, 0)
        forward(2 * m + 1, 1)
        return 0

    def two_backward(m, _):
        backward(2 * m, 0)
        backward(2 * m + 1, 1)
        return 0

    lax.fori_loop(0, layers // 2, two_forward, 0)
    backward(0, 0, top=True)
    backward(1, 1)
    lax.fori_loop(1, layers // 2, two_backward, 0)
    for b in range(2):
        rows = slice(b * BLK, (b + 1) * BLK)
        back = aggregate(layers % 2, b).astype(BF16)
        grad_initial[0, rows, :] = grad_initial[0, rows, :] + back.astype(F32)


def run_layers(scale, betas, pieces, weights):
    vmem = pl.BlockSpec(memory_space=pltpu.VMEM)
    nodes, width = 2048, 256
    return pl.pallas_call(
        functools.partial(layers_kernel, scale, betas),
        in_specs=[vmem] * (len(pieces) + len(weights)),
        out_specs=[vmem, vmem],
        out_shape=[
            jax.ShapeDtypeStruct((1, 256, width), F32),
            jax.ShapeDtypeStruct((4, 64, width), BF16),
        ],
        scratch_shapes=[
            pltpu.VMEM((nodes, width), F32),
            pltpu.VMEM((4, width, width), BF16),
            pltpu.VMEM((8, BLK), jnp.int32),
            pltpu.SMEM((8, BLK), jnp.int32),
            pltpu.VMEM((nodes, width), BF16),
            pltpu.VMEM((nodes, width), BF16),
            pltpu.VMEM((4, nodes, width), BF16),
            pltpu.VMEM((4, nodes, width), F32),
            pltpu.VMEM((nodes, width), BF16),
            pltpu.VMEM((BLK, width), F32),
            pltpu.SemaphoreType.DMA,
        ],
        compiler_params=pltpu.CompilerParams(vmem_limit_bytes=40 * 1024 * 1024),
        cost_estimate=pl.CostEstimate(flops=9_000_000_000, bytes_accessed=6_000_000, transcendentals=0),
        name="layers",
    )(*pieces, *weights)


def onward(v):
    route = [(i, (i + 2) % 8 if i % 2 == 0 else (i - 2) % 8) for i in range(8)]
    return lax.ppermute(v, "dom", route)


def other_core(v):
    return lax.ppermute(v, "dom", [(i, i ^ 1) for i in range(8)])


def to_phase(v, n):
    return lax.ppermute(v, "phase", [(i, (i + n) % 4) for i in range(4)])


def across(v):
    route = [(i, (i + 2) % 8 - 1 if i % 2 else (i - 2) % 8 + 1) for i in range(8)]
    return lax.ppermute(v, "dom", route)


def gather(own, w):
    near, near_too = onward(own), across(own)
    partner = other_core(own)
    weights = [w] + [to_phase(w, n) for n in (1, 2, 3)]
    early, *weights = lax.optimization_barrier((near, *weights))
    far = onward(early)
    pieces = [own, partner, near, near_too, far, other_core(far), other_core(near_too), other_core(near)]
    return pieces, weights


def local(initial, block_cols, block_tiles, layer_weights, cotangent):
    layers = lax.axis_size("phase")
    nodes_all = 4 * 2048 * lax.axis_size("dp")
    scale = 1.0 / math.sqrt(nodes_all)
    betas = [math.log(THETA / (l + 1) + 1.0) for l in range(layers)]
    spans, rows = block_tiles.shape[:2]
    tiles = block_tiles.reshape(spans, rows * NZB * BLK, BLK)
    own = pack(tiles, initial, cotangent, block_cols)
    pieces, weights = gather(own, layer_weights)
    grad_initial, parts = run_layers(scale, betas, pieces, weights)
    mine = parts[0].astype(F32)
    for n in (1, 2, 3):
        mine = mine + to_phase(parts[n], n).astype(F32)
    mine = mine.astype(BF16)
    mine = jnp.broadcast_to(mine[None], (8,) + mine.shape)
    mine = jnp.sum(lax.all_to_all(mine, "dp", 0, 0, tiled=True).astype(F32), axis=0)
    dom = lax.axis_index("dom")
    sent = mine.astype(BF16)
    held = [lax.ppermute(sent, "dom", [(i, i ^ n) for i in range(8)]).astype(F32) for n in (2, 3, 1)]
    held = [mine] + held
    by_bits = {0: held[0], 2: held[1], 3: held[2], 1: held[3]}
    far_chip, far_core = lax.bitwise_and(dom, 2) != 0, lax.bitwise_and(dom, 1) != 0
    rows = []
    for quarter in (0, 2, 1, 3):
        chip = [jnp.where(far_chip, by_bits[quarter ^ 2 ^ n], by_bits[quarter ^ n]) for n in (0, 1)]
        rows.append(jnp.where(far_core, chip[1], chip[0]))
    return grad_initial, jnp.concatenate(rows, axis=0)[None]


def solution(mesh):
    placed = (
        P("dp", "dom", None),
        P("dp", "dom", None),
        P("dp", "dom", None, None, None),
        P("phase", None, None),
        P("dp", "dom", None),
    )
    return jax.shard_map(
        local,
        mesh=mesh,
        in_specs=placed,
        out_specs=(P(("dp", "phase"), "dom", None), P("phase", None, None)),
        check_vma=False,
    )
```

```python
import functools
import math

import jax
import jax.numpy as jnp
from jax import lax
from jax.experimental import pallas as pl
from jax.experimental.pallas import tpu as pltpu
from jax.sharding import PartitionSpec as P

ALPHA = 0.1
THETA = 0.5
BLK = 128
NZB = 5
GELU_C = math.sqrt(2.0 / math.pi)
GELU_B = 0.044715
ROWS = 2 * BLK
TILE_ROWS = 2 * NZB * BLK
START = TILE_ROWS
COT = START + 2 * ROWS
COLS = COT + 2 * ROWS
PIECE = COLS + 16
CHUNK = 4
LAG = 8
GELU_C = math.sqrt(2.0 / math.pi)
GELU_B = 0.044715
HEAD_TILES = 7
TAIL_START = (2 * NZB - HEAD_TILES) * BLK
TAIL_COLS = TAIL_START + 512
CHUNK = 4
LAG = 8
BF16 = jnp.bfloat16
F32 = jnp.float32


def pack_kernel(tiles, initial, cotangent, cols, piece, start, cot, sems):
    span = lax.axis_index("phase")
    copies = [
        (initial.at[span], start),
        (cotangent.at[span], cot),
        (tiles.at[span], piece.at[pl.ds(0, TILE_ROWS)]),
    ]
    started = [pltpu.make_async_copy(a, b, sems.at[n]) for n, (a, b) in enumerate(copies)]
    for c in started:
        c.start()
    lane = lax.broadcasted_iota(jnp.int32, (16, BLK), 1)
    vec = jnp.zeros((16, BLK), F32)
    for b in range(2):
        for k in range(NZB):
            vec = jnp.where(lane == b * NZB + k, cols[span, b, k].astype(F32), vec)
    piece[COLS : COLS + 16, :] = vec.astype(BF16)
    for copy, base, array in ((started[0], START, start), (started[1], COT, cot)):
        copy.wait()
        piece[base : base + ROWS, :] = array[:, :BLK]
        piece[base + ROWS : base + 2 * ROWS, :] = array[:, BLK:]
    started[2].wait()


def pack(tiles, initial, cotangent, cols):
    any_spec = pl.BlockSpec(memory_space=pl.ANY)
    return pl.pallas_call(
        pack_kernel,
        in_specs=[any_spec, any_spec, any_spec, pl.BlockSpec(memory_space=pltpu.SMEM)],
        out_specs=pl.BlockSpec(memory_space=pltpu.VMEM),
        out_shape=pltpu.VMEM((PIECE, BLK), BF16),
        scratch_shapes=[
            pltpu.VMEM((ROWS, 2 * BLK), BF16),
            pltpu.VMEM((ROWS, 2 * BLK), BF16),
            pltpu.SemaphoreType.DMA((3,)),
        ],
        name="pack",
    )(*[pltpu.with_memory_space_constraint(a, pltpu.HBM) for a in (tiles, initial, cotangent)], cols)


def dot(a, b, dims):
    return lax.dot_general(a, b, (dims, ((), ())), preferred_element_type=F32)


def layers_kernel(scale, betas, *refs):
    layers = len(betas)
    pieces, weights = refs[:8], refs[8 : 8 + layers]
    grad_initial, grad_weights = refs[8 + layers : 10 + layers]
    start, weight, cols_int, cols, h_even, h_odd, mixes, slopes, dpre, dw, sem = refs[10 + layers :]

    hidden = (h_even, h_odd)

    def piece(n, low, rows):
        return pieces[n][low : low + rows, :]

    dom = lax.axis_index("dom")
    phase = lax.axis_index("phase")
    x, core = dom // 2, dom % 2
    for n in range(layers):
        weight[(phase - n + layers) % layers] = weights[n][0]
    way = 1 - 2 * core
    for n in range(8):
        j = piece(n, COLS, 16).astype(F32).astype(jnp.int32)
        chip = lax.bitwise_and(way * (x - lax.shift_right_logical(j, 2)) + 4, 3)
        side = lax.bitwise_xor(lax.bitwise_and(lax.shift_right_logical(j, 1), 1), core)
        place = chip * 4 + side * 2 + lax.bitwise_and(j, 1)
        cols_int[n : n + 1, :] = (place * BLK)[:1]
    to_scalars = pltpu.make_async_copy(cols_int, cols, sem)
    to_scalars.start()
    for n in range(8):
        for half in range(2):
            part = piece(n, START + ROWS * half, ROWS)
            lanes = slice(BLK * half, BLK * (half + 1))
            h_even[ROWS * n : ROWS * (n + 1), lanes] = part
            start[ROWS * n : ROWS * (n + 1), lanes] = ALPHA * part.astype(F32)
    to_scalars.wait()

    def tile(i, k):
        return piece(i // 2, ((i % 2) * NZB + k) * BLK, BLK)

    def aggregate(src, i):
        blocks = [hidden[src][i * BLK : (i + 1) * BLK, :]]
        for k in range(1, NZB):
            j = pl.multiple_of(cols[i // 2, (i % 2) * NZB + k], BLK)
            blocks.append(hidden[src][pl.ds(j, BLK), :])
        lhs = jnp.concatenate([tile(i, k) for k in range(NZB)], axis=1)
        return (1.0 - ALPHA) * dot(lhs, jnp.concatenate(blocks, axis=0), ((1,), (0,)))

    blocks_all = start.shape[0] // BLK

    def pipeline(first, second, third):
        held = {}
        for s in range(blocks_all + LAG):
            if s < blocks_all:
                first(s)
            if s < blocks_all + CHUNK and s >= CHUNK and s % CHUNK == 0:
                held[s // CHUNK - 1] = second(s // CHUNK - 1)
            i = s - LAG
            if 0 <= i < blocks_all:
                product = held[i // CHUNK]
                third(i, product[(i % CHUNK) * BLK : (i % CHUNK + 1) * BLK, :])

    def pick(values, l):
        if isinstance(l, int):
            return values[l]
        out = jnp.float32(values[0])
        for n in range(1, len(values)):
            out = jnp.where(l == n, jnp.float32(values[n]), out)
        return out

    def forward(l, src):
        dst = 1 - src
        beta = pick(betas, l)
        w = weight[l]

        def first(i):
            rows = slice(i * BLK, (i + 1) * BLK)
            mixes[l, rows, :] = (aggregate(src, i) + start[rows, :]).astype(BF16)

        def second(c):
            return dot(mixes[l, c * CHUNK * BLK : (c + 1) * CHUNK * BLK, :], w, ((1,), (0,)))

        def third(i, product):
            rows = slice(i * BLK, (i + 1) * BLK)
            pre = (1.0 - beta) * mixes[l, rows, :].astype(F32) + beta * product
            square = pre * pre
            t = jnp.tanh(pre * (GELU_C + (GELU_C * GELU_B) * square))
            half = 0.5 + 0.5 * t
            out = pre * half
            hidden[dst][rows, :] = out.astype(BF16)
            slopes[l, rows, :] = half + out * (1.0 - half) * (
                2.0 * GELU_C + (6.0 * GELU_C * GELU_B) * square
            )

        pipeline(first, second, third)
        return 0

    def backward(step, src, top=False):
        l = layers - 1 - step
        dst = 1 - src
        beta = pick(betas, l)
        w = weight[l]

        def first(i):
            rows = slice(i * BLK, (i + 1) * BLK)
            if top:
                low = COT + (i % 2) * BLK
                back = jnp.concatenate([piece(i // 2, low, BLK), piece(i // 2, low + ROWS, BLK)], axis=1)
            else:
                back = aggregate(src, i).astype(BF16)
            dpre[rows, :] = (slopes[l, rows, :] * back.astype(F32)).astype(BF16)

        def second(c):
            return dot(dpre[c * CHUNK * BLK : (c + 1) * CHUNK * BLK, :], w, ((1,), (1,)))

        def third(i, product):
            rows = slice(i * BLK, (i + 1) * BLK)
            dmix = (1.0 - beta) * dpre[rows, :].astype(F32) + beta * product
            hidden[dst][rows, :] = dmix.astype(BF16)

        pipeline(first, second, third)
        term = ALPHA * hidden[dst][0:256, :].astype(F32)
        grad_initial[0] = term if top else grad_initial[0] + term
        lanes = pl.ds(pl.multiple_of(core * BLK, BLK), BLK)
        dw[...] = (beta * scale) * dot(mixes[l, :, lanes], dpre[...], ((0,), (0,)))
        grad_weights[(l - phase + layers) % layers] = dw[pl.ds(pl.multiple_of(x % 2 * 64, 64), 64), :].astype(BF16)
        return 0

    def two_forward(m, _):
        forward(2 * m, 0)
        forward(2 * m + 1, 1)
        return 0

    def two_backward(m, _):
        backward(2 * m, 0)
        backward(2 * m + 1, 1)
        return 0

    lax.fori_loop(0, layers // 2, two_forward, 0)
    backward(0, 0, top=True)
    backward(1, 1)
    lax.fori_loop(1, layers // 2, two_backward, 0)
    for b in range(2):
        rows = slice(b * BLK, (b + 1) * BLK)
        back = aggregate(layers % 2, b).astype(BF16)
        grad_initial[0, rows, :] = grad_initial[0, rows, :] + back.astype(F32)


def run_layers(scale, betas, pieces, weights):
    vmem = pl.BlockSpec(memory_space=pltpu.VMEM)
    nodes, width = 2048, 256
    return pl.pallas_call(
        functools.partial(layers_kernel, scale, betas),
        in_specs=[vmem] * (len(pieces) + len(weights)),
        out_specs=[vmem, vmem],
        out_shape=[
            jax.ShapeDtypeStruct((1, 256, width), F32),
            jax.ShapeDtypeStruct((4, 64, width), BF16),
        ],
        scratch_shapes=[
            pltpu.VMEM((nodes, width), F32),
            pltpu.VMEM((4, width, width), BF16),
            pltpu.VMEM((8, BLK), jnp.int32),
            pltpu.SMEM((8, BLK), jnp.int32),
            pltpu.VMEM((nodes, width), BF16),
            pltpu.VMEM((nodes, width), BF16),
            pltpu.VMEM((4, nodes, width), BF16),
            pltpu.VMEM((4, nodes, width), F32),
            pltpu.VMEM((nodes, width), BF16),
            pltpu.VMEM((BLK, width), F32),
            pltpu.SemaphoreType.DMA,
        ],
        compiler_params=pltpu.CompilerParams(vmem_limit_bytes=40 * 1024 * 1024),
        cost_estimate=pl.CostEstimate(flops=9_000_000_000, bytes_accessed=6_000_000, transcendentals=0),
        name="layers",
    )(*pieces, *weights)


def onward(v):
    route = [(i, (i + 2) % 8 if i % 2 == 0 else (i - 2) % 8) for i in range(8)]
    return lax.ppermute(v, "dom", route)


def other_core(v):
    return lax.ppermute(v, "dom", [(i, i ^ 1) for i in range(8)])


def to_phase(v, n):
    return lax.ppermute(v, "phase", [(i, (i + n) % 4) for i in range(4)])


def across(v):
    route = [(i, (i + 2) % 8 - 1 if i % 2 else (i - 2) % 8 + 1) for i in range(8)]
    return lax.ppermute(v, "dom", route)


def gather(own, w):
    near, near_too = onward(own), across(own)
    partner = other_core(own)
    weights = [w] + [to_phase(w, n) for n in (1, 2, 3)]
    early, *weights = lax.optimization_barrier((near, *weights))
    far = onward(early)
    pieces = [own, partner, near, near_too, far, other_core(far), other_core(near_too), other_core(near)]
    return pieces, weights


def local(initial, block_cols, block_tiles, layer_weights, cotangent):
    layers = lax.axis_size("phase")
    nodes_all = 4 * 2048 * lax.axis_size("dp")
    scale = 1.0 / math.sqrt(nodes_all)
    betas = [math.log(THETA / (l + 1) + 1.0) for l in range(layers)]
    spans, rows = block_tiles.shape[:2]
    tiles = block_tiles.reshape(spans, rows * NZB * BLK, BLK)
    own = pack(tiles, initial, cotangent, block_cols)
    pieces, weights = gather(own, layer_weights)
    grad_initial, parts = run_layers(scale, betas, pieces, weights)
    mine = parts[0].astype(F32)
    for n in (1, 2, 3):
        mine = mine + to_phase(parts[n], n).astype(F32)
    mine = mine.astype(BF16)
    mine = jnp.broadcast_to(mine[None], (8,) + mine.shape)
    mine = jnp.sum(lax.all_to_all(mine, "dp", 0, 0, tiled=True).astype(F32), axis=0)
    dom = lax.axis_index("dom")
    sent = lax.optimization_barrier(mine.astype(BF16))
    held = [lax.ppermute(sent, "dom", [(i, i ^ n) for i in range(8)]).astype(F32) for n in (2, 3, 1)]
    held = [sent.astype(F32)] + held
    by_bits = {0: held[0], 2: held[1], 3: held[2], 1: held[3]}
    far_chip, far_core = lax.bitwise_and(dom, 2) != 0, lax.bitwise_and(dom, 1) != 0
    rows = []
    for quarter in (0, 2, 1, 3):
        chip = [jnp.where(far_chip, by_bits[quarter ^ 2 ^ n], by_bits[quarter ^ n]) for n in (0, 1)]
        rows.append(jnp.where(far_core, chip[1], chip[0]))
    return grad_initial, jnp.concatenate(rows, axis=0)[None]


def solution(mesh):
    placed = (
        P("dp", "dom", None),
        P("dp", "dom", None),
        P("dp", "dom", None, None, None),
        P("phase", None, None),
        P("dp", "dom", None),
    )
    return jax.shard_map(
        local,
        mesh=mesh,
        in_specs=placed,
        out_specs=(P(("dp", "phase"), "dom", None), P("phase", None, None)),
        check_vma=False,
    )
```
